128 devices in a mesh: leaf: 32 (over y_lo, x, z), pts: 4 (over y_hi, core).
Axes of the slice: x: 4, y: 4 (y_hi: 2, y_lo: 2; y = y_hi * 2 + y_lo), z: 4, core: 2. Of those that a mesh axis runs over, the one named last changes fastest.
Arguments:
- points_rhs: float32 [524288, 512], P(('leaf', 'pts')), may hold values from -6 to 6
- order: int32 [128, 4096], P(('leaf', 'pts')), may hold values from 0 to 4095, each once within a row
- basis: float32 [524288, 256], P(('leaf', 'pts')), may hold values from -0.046875 to 0.046875
- near_blocks: float32 [8192, 128, 128], P(('leaf', 'pts')), may hold values from -0.375 to 0.375
- near_pairs: int32 [8192, 2], P(('leaf', 'pts')), may hold values from 0 to 33, as said below
- transfer: float32 [32, 4, 256, 256], P('leaf'), may hold values from -0.375 to 0.375
- coupling: float32 [32, 5, 256, 256], P('leaf'), may hold values from -0.375 to 0.375
Outputs:
- product: float32 [524288, 512], P(('leaf', 'pts'))
The draws below stay inside these ranges and needn't reach their ends.
Inputs may be any that keep to these rules, and one draw needn't show every extreme that they name: `near_pairs`: each device's 64 pairs (r, c) have r in 0 .. 31 and c in r .. r + 2; every row block appears; row block 0 appears with column block 0 and the last row block with the last column block. `order`: each device's row is a permutation of 0 .. 4095.
All inputs are finite; a program needn't handle non-finite values.
Results may differ from the reference program's by a relative error of at most 0.0003.
Values sent between devices are 32-bit elements; how exact they have to be, the bound alone decides.
A program may use at most 192 MiB of HBM per device.

```python
import jax
import jax.numpy as jnp
from jax import lax

ROWS = 4096
RHS = 512
RANK = 256
BLK = 128
LEVELS = 5
NBLK = 64
DEVS = 128
POINTS = 524288
N_LEAF = 32
N_PTS = 4


def draw_near_pairs(key, part):
    key = jax.random.fold_in(key, 7)
    row_blocks = ROWS // BLK

    def one_device(dev_key):
        key_first, key_rest, key_offset, key_shuffle = jax.random.split(dev_key, 4)
        first_rows = jnp.arange(row_blocks, dtype=jnp.int32)
        first_offsets = jax.random.randint(key_first, (row_blocks,), 0, 3).astype(jnp.int32)
        first_offsets = first_offsets.at[0].set(0).at[row_blocks - 1].set(2)
        more_rows = jax.random.randint(key_rest, (row_blocks,), 0, row_blocks).astype(jnp.int32)
        more_offsets = jax.random.randint(key_offset, (row_blocks,), 0, 3).astype(jnp.int32)
        row_list = jnp.concatenate([first_rows, more_rows])
        col_list = row_list + jnp.concatenate([first_offsets, more_offsets])
        shuffle = jax.random.permutation(key_shuffle, 2 * row_blocks)
        return jnp.stack([row_list[shuffle], col_list[shuffle]], 1)
    dev_keys = jax.random.split(key, DEVS)
    return jax.vmap(one_device)(dev_keys).reshape(DEVS * NBLK, 2).astype(jnp.int32)


def levels(rng, dims, pieces, least, top_value):
    factor_of, own = 1.0, jax.random.fold_in(rng, 6)
    for position, parts in pieces:
        draws = jnp.exp(jax.random.uniform(jax.random.fold_in(own, position), (parts,), jnp.float32, least / len(pieces), top_value / len(pieces)))
        factor_of = factor_of * jnp.repeat(draws, dims[position] // parts).reshape([-1 if axis == position else 1 for axis in range(len(dims))])
    return factor_of


def gaussian(stream_key, shape, deviation, bound, pieces=(), kind=jnp.bfloat16):
    result = deviation * jax.random.normal(stream_key, shape, jnp.float32)
    if pieces:
        result = result * levels(stream_key, shape, pieces, -0.22, 0.18)
    return jnp.clip(result, -bound, bound).astype(kind)


def setup_inputs(seed: int = 0) -> dict:
    seeds = jax.random.split(jax.random.key(seed), 8)
    return {
        "points_rhs": gaussian(seeds[0], (POINTS, RHS), 1.0, 6.0, ((0, 128),), jnp.float32),
        "order": jax.vmap(lambda own: jax.random.permutation(own, ROWS))(jax.random.split(seeds[1], DEVS)).reshape((DEVS, ROWS)).astype(jnp.int32),
        "basis": gaussian(seeds[2], (POINTS, RANK), (ROWS * N_PTS) ** -0.5, 0.046875, ((0, 128),), jnp.float32),
        "near_blocks": gaussian(seeds[3], (DEVS * NBLK, BLK, BLK), (2 * BLK) ** -0.5, 0.375, ((0, 128),), jnp.float32),
        "near_pairs": draw_near_pairs(jax.random.fold_in(seeds[7], 71), 0),
        "transfer": gaussian(seeds[5], (N_LEAF, LEVELS - 1, RANK, RANK), RANK ** -0.5, 0.375, ((0, 32),), jnp.float32),
        "coupling": gaussian(seeds[6], (N_LEAF, LEVELS, RANK, RANK), RANK ** -0.5, 0.375, ((0, 32),), jnp.float32),
    }


HIGHEST = lax.Precision.HIGHEST


def sibling(values, bit_pos):
    count = values.shape[0]
    step_size = 2 ** bit_pos
    shaped = values.reshape((count // (2 * step_size), 2, step_size) + values.shape[1:])
    return shaped[:, ::-1].reshape(values.shape)


def near_device(inputs):
    tree_rows, lower_rim, upper_rim, blocks, pairs = inputs
    row_blocks = tree_rows.shape[0] // BLK
    padded = jnp.concatenate([lower_rim, tree_rows, upper_rim], 0).reshape(row_blocks + 2, BLK, -1)
    picked = padded[pairs[:, 1]]
    terms = jnp.einsum("kij,kjr->kir", blocks, picked, precision=HIGHEST)
    onehot = (pairs[:, 0][None, :] == jnp.arange(row_blocks, dtype=jnp.int32)[:, None]).astype(jnp.float32)
    summed = jnp.dot(onehot, terms.reshape(terms.shape[0], -1), precision=HIGHEST)
    return summed.reshape(tree_rows.shape)


def place_rows(tree_out, order_row):
    return jnp.zeros_like(tree_out).at[order_row].set(tree_out)


def reference(points_rhs, order, basis, near_blocks, near_pairs, transfer, coupling):
    inputs = points_rhs.reshape(N_LEAF, N_PTS, ROWS, RHS)
    orders = order.reshape(N_LEAF, N_PTS, ROWS)
    tree_rows = jnp.take_along_axis(inputs, orders[..., None], axis=2)
    basis_rows = basis.reshape(N_LEAF, N_PTS, ROWS, RANK)
    coefficient = jnp.einsum("lpik,lpir->lkr", basis_rows, tree_rows, precision=HIGHEST)
    coupled = []
    for level_idx in range(LEVELS):
        sibling_c = sibling(coefficient, level_idx)
        coupled.append(jnp.einsum("lij,ljr->lir", coupling[:, level_idx], sibling_c, precision=HIGHEST))
        if level_idx < LEVELS - 1:
            lifted = jnp.einsum("lji,ljr->lir", transfer[:, level_idx], coefficient, precision=HIGHEST)
            coefficient = lifted + sibling(lifted, level_idx)
    downward = coupled[LEVELS - 1]
    for level_idx in range(LEVELS - 2, -1, -1):
        downward = coupled[level_idx] + jnp.einsum("lij,ljr->lir", transfer[:, level_idx], downward, precision=HIGHEST)
    far_part = jnp.einsum("lpik,lkr->lpir", basis_rows, downward, precision=HIGHEST)
    zero_rim = jnp.zeros((N_LEAF, 1, BLK, RHS), jnp.float32)
    lower_rim = jnp.concatenate([zero_rim, tree_rows[:, :-1, ROWS - BLK:]], 1)
    upper_rim = jnp.concatenate([tree_rows[:, 1:, :BLK], zero_rim], 1)
    device_count = N_LEAF * N_PTS
    near_part = lax.map(near_device, (tree_rows.reshape(device_count, ROWS, RHS),
                                      lower_rim.reshape(device_count, BLK, RHS),
                                      upper_rim.reshape(device_count, BLK, RHS),
                                      near_blocks.reshape(device_count, NBLK, BLK, BLK),
                                      near_pairs.reshape(device_count, NBLK, 2)))
    tree_out = near_part + far_part.reshape(device_count, ROWS, RHS)
    placed = jax.vmap(place_rows)(tree_out, orders.reshape(device_count, ROWS))
    return placed.reshape(POINTS, RHS)
```

```python
import functools

import jax
import jax.numpy as jnp
from jax import lax
from jax.experimental import pallas as pl
from jax.experimental.pallas import tpu as pltpu
from jax.sharding import PartitionSpec as P

MESH = pl.DeviceIdType.MESH
F32, BF16 = jnp.float32, jnp.bfloat16
LANES, SUB = 128, 8
MIB = 2**20


def split(x):
    hi = x.astype(BF16)
    return hi, (x - hi.astype(F32)).astype(BF16)


def dot(a, b):
    return jnp.dot(a, b, preferred_element_type=F32)


def dot_t(a, b):
    return lax.dot_general(a, b, (((1,), (1,)), ((), ())), preferred_element_type=F32)


def three(mul, a, b):
    (ah, al), (bh, bl) = a, b
    return mul(ah, bh) + (mul(ah, bl) + mul(al, bh))


def gather_kernel(addr, pairs, x_hbm, basis_hbm, near_hbm, c_out, edge_out, th_hbm, tl_hbm, ah_hbm, al_hbm,
                  xv, bv, nv, band, bth, btl, rows_f, thv, tlv, acc, ahv, alv, in_sem, out_sem, a_sem):
    rows, rank = bv.shape
    cols = thv.shape[1]
    tiles = cols // LANES
    chunk = rows_f.shape[0] // tiles
    chunks = rows // chunk
    blocks, size = nv.shape[0], nv.shape[1]
    row_blocks = rows // size
    in_b = pltpu.make_async_copy(basis_hbm, bv, in_sem.at[0])
    in_n = pltpu.make_async_copy(near_hbm, nv, in_sem.at[1])
    in_x = pltpu.make_async_copy(x_hbm, xv, in_sem.at[2])
    in_b.start()
    in_n.start()
    in_x.start()

    @pl.loop(0, row_blocks)
    def _(r):
        band[pl.ds(3 * r, 3)] = jnp.zeros((3, size, size), F32)

    acc[...] = jnp.zeros_like(acc)
    in_b.wait()

    @pl.loop(0, rows // 256)
    def _(i):
        at = pl.multiple_of(i * 256, 256)
        h, l = split(bv[pl.ds(at, 256), :].T)
        bth[:, pl.ds(at, 256)] = h
        btl[:, pl.ds(at, 256)] = l

    in_n.wait()

    @pl.loop(0, blocks)
    def _(k):
        r = pairs[2 * k]
        slot = 2 * r + pairs[2 * k + 1]
        band[slot] = band[slot] + nv[k]

    @pl.loop(0, row_blocks)
    def _(r):
        for o in range(3):
            h, l = split(band[3 * r + o])
            ahv[r, :, o * size:(o + 1) * size] = h
            alv[r, :, o * size:(o + 1) * size] = l

    out_ah = pltpu.make_async_copy(ahv, ah_hbm, a_sem.at[0])
    out_al = pltpu.make_async_copy(alv, al_hbm, a_sem.at[1])
    out_ah.start()
    out_al.start()
    in_x.wait()

    @pl.loop(0, chunks)
    def _(i):
        step = 32

        @pl.loop(0, chunk // step)
        def _(g):
            first = i * chunk + g * step
            vals = [xv[pl.ds(addr[first + u], tiles, stride=SUB), :] for u in range(step)]
            for u in range(step):
                to = g * (step * tiles) + (u // SUB) * (SUB * tiles) + u % SUB
                rows_f[pl.ds(to, tiles, stride=SUB), :] = vals[u]

        at = pl.multiple_of(i * chunk, chunk)
        for j in range(tiles):
            part = jnp.concatenate(
                [rows_f[(g * tiles + j) * SUB:(g * tiles + j + 1) * SUB, :] for g in range(chunk // SUB)], axis=0)
            h, l = split(part)
            thv[pl.ds(at, chunk), j * LANES:(j + 1) * LANES] = h
            tlv[pl.ds(at, chunk), j * LANES:(j + 1) * LANES] = l

            @pl.when(i == 0)
            def _():
                edge_out[0, :, j * LANES:(j + 1) * LANES] = part[:size]

            @pl.when(i == chunks - 1)
            def _():
                edge_out[1, :, j * LANES:(j + 1) * LANES] = part[chunk - size:]

        t = thv[pl.ds(at, chunk), :], tlv[pl.ds(at, chunk), :]
        b = bth[:, pl.ds(at, chunk)], btl[:, pl.ds(at, chunk)]
        acc[...] += three(dot, b, t)
        pltpu.make_async_copy(thv.at[pl.ds(at, chunk)], th_hbm.at[pl.ds(at, chunk)], out_sem.at[0, i]).start()
        pltpu.make_async_copy(tlv.at[pl.ds(at, chunk)], tl_hbm.at[pl.ds(at, chunk)], out_sem.at[1, i]).start()

    for j in range(tiles):
        c_out[j * LANES:(j + 1) * LANES, :] = acc[:, j * LANES:(j + 1) * LANES].T
    out_ah.wait()
    out_al.wait()

    @pl.loop(0, chunks)
    def _(i):
        at = pl.multiple_of(i * chunk, chunk)
        pltpu.make_async_copy(thv.at[pl.ds(at, chunk)], th_hbm.at[pl.ds(at, chunk)], out_sem.at[0, i]).wait()
        pltpu.make_async_copy(tlv.at[pl.ds(at, chunk)], tl_hbm.at[pl.ds(at, chunk)], out_sem.at[1, i]).wait()


def gather_call(addr, pairs, x, basis, near):
    rows, rank = basis.shape
    cols = x.shape[0] * LANES // rows
    tiles = cols // LANES
    size = near.shape[1]
    row_blocks = rows // size
    chunk = min(512, rows)
    chunks = rows // chunk
    smem, hbm, vmem = (pl.BlockSpec(memory_space=s) for s in (pltpu.SMEM, pl.ANY, pltpu.VMEM))
    shape = jax.ShapeDtypeStruct
    return pl.pallas_call(
        gather_kernel,
        out_shape=(shape((cols, rank), F32), shape((2, size, cols), F32), shape((rows, cols), BF16), shape((rows, cols), BF16),
                   shape((row_blocks, size, 3 * size), BF16), shape((row_blocks, size, 3 * size), BF16)),
        in_specs=[smem, smem, hbm, hbm, hbm],
        out_specs=(vmem, vmem, hbm, hbm, hbm, hbm),
        scratch_shapes=[
            pltpu.VMEM(x.shape, F32), pltpu.VMEM(basis.shape, F32), pltpu.VMEM(near.shape, F32),
            pltpu.VMEM((3 * row_blocks, size, size), F32),
            pltpu.VMEM((rank, rows), BF16), pltpu.VMEM((rank, rows), BF16),
            pltpu.VMEM((chunk * tiles, LANES), F32),
            pltpu.VMEM((rows, cols), BF16), pltpu.VMEM((rows, cols), BF16),
            pltpu.VMEM((rank, cols), F32),
            pltpu.VMEM((row_blocks, size, 3 * size), BF16), pltpu.VMEM((row_blocks, size, 3 * size), BF16),
            pltpu.SemaphoreType.DMA((3,)), pltpu.SemaphoreType.DMA((2, chunks)), pltpu.SemaphoreType.DMA((2,)),
        ],
        compiler_params=pltpu.CompilerParams(vmem_limit_bytes=56 * MIB),
        name="gather_compress",
    )(addr, pairs, x, basis, near)


def tree_kernel(levels, c_in, edge_in, th_hbm, tl_hbm, ah_hbm, al_hbm, t_in, g_in, d_out, near_hbm,
                ph, pl_, ahv, alv, nv, wth, wtl, wgh, wgl, rs1, stage, rs2, cbuf, lbuf, lrecv, crecv, coup, dbuf, erecv,
                in_sem, n_sem, rs_send, rs_recv, l_send, l_recv, c_send, c_recv, d_send, d_recv, e_send, e_recv):
    rows, cols = nv.shape
    rank = c_in.shape[1]
    row_blocks, size = ahv.shape[0], ahv.shape[1]
    width = cbuf.shape[1]
    leaf, p = lax.axis_index("leaf"), lax.axis_index("pts")
    parts = lax.axis_size("pts")
    core, far_chip = (leaf, p ^ 1), (leaf, p ^ 2)
    following, before = (leaf, lax.rem(p + 1, parts)), (leaf, lax.rem(p + parts - 1, parts))
    siblings = [(leaf ^ (1 << l), p) for l in range(levels)]

    copies = [
        pltpu.make_async_copy(th_hbm, ph.at[pl.ds(size, rows)], in_sem.at[0]),
        pltpu.make_async_copy(tl_hbm, pl_.at[pl.ds(size, rows)], in_sem.at[1]),
        pltpu.make_async_copy(ah_hbm, ahv, in_sem.at[2]),
        pltpu.make_async_copy(al_hbm, alv, in_sem.at[3]),
    ]

    barrier = pltpu.get_barrier_semaphore()
    greeted = [core, far_chip, (leaf, p ^ 3)] + siblings
    for other in greeted:
        pl.semaphore_signal(barrier, inc=1, device_id=other, device_id_type=MESH)
    for copy in copies:
        copy.start()
    pl.semaphore_wait(barrier, len(greeted))

    def send(src, dst, to, send_sem, recv_sem):
        copy = pltpu.make_async_remote_copy(
            src_ref=src, dst_ref=dst, send_sem=send_sem, recv_sem=recv_sem, device_id=to, device_id_type=MESH)
        copy.start()
        return copy

    def block(ref, q):
        return ref.at[pl.ds(pl.multiple_of(q * width, width), width)]

    started = []
    s0 = send(block(c_in, p ^ 3), rs1.at[0], core, rs_send.at[0], rs_recv.at[0])
    s1 = send(block(c_in, p ^ 1), rs1.at[1], core, rs_send.at[1], rs_recv.at[1])

    def weights(l):
        if l < levels - 1:
            wth[l], wtl[l] = split(t_in[l])
        wgh[l], wgl[l] = split(g_in[l])

    weights(0)
    s0.wait_recv()
    stage[...] = block(c_in, p ^ 2)[...] + rs1[0]
    s2 = send(stage, rs2, far_chip, rs_send.at[2], rs_recv.at[2])
    for l in range(1, levels):
        weights(l)
    s1.wait_recv()
    cbuf[0] = block(c_in, p)[...] + rs1[1]
    started += [s0, s1, s2]

    def near(first, count):
        @pl.loop(first, first + count)
        def _(r):
            at = pl.multiple_of(r * size, size)
            span = pl.ds(at, 3 * size)
            nv[pl.ds(at, size), :] = three(dot, (ahv[r], alv[r]), (ph[span, :], pl_[span, :]))

        if count:
            out = pltpu.make_async_copy(
                nv.at[pl.ds(first * size, count * size)], near_hbm.at[pl.ds(first * size, count * size)], n_sem.at[first])
            out.start()
            outs.append(out)

    outs = []
    inner = row_blocks - 2
    cuts = [1 + inner * i // (levels + 1) for i in range(levels + 2)]

    def near_step(i):
        near(cuts[i], cuts[i + 1] - cuts[i])

    for copy in copies:
        copy.wait()
    near_step(0)
    s2.wait_recv()
    cbuf[0] = cbuf[0] + rs2[...]

    edges = []
    couples = []
    for l in range(levels - 1):
        lifted = three(dot, split(cbuf[l]), (wth[l], wtl[l]))
        lbuf[l] = lifted
        a = send(lbuf.at[l], lrecv.at[l], siblings[l], l_send.at[l], l_recv.at[l])
        b = send(cbuf.at[l], crecv.at[l], siblings[l], c_send.at[l], c_recv.at[l])
        if l == 0:
            edges.append(send(edge_in.at[1], erecv.at[0], following, e_send.at[0], e_recv.at[0]))
            edges.append(send(edge_in.at[0], erecv.at[1], before, e_send.at[1], e_recv.at[1]))
        couples.append(b)
        started += [a, b]
        near_step(1 + l)
        a.wait_recv()
        cbuf[l + 1] = lifted + lrecv[l]
    top = levels - 1
    b = send(cbuf.at[top], crecv.at[top], siblings[top], c_send.at[top], c_recv.at[top])
    started.append(b)
    for l in range(levels - 1):
        couples[l].wait_recv()
        coup[l] = three(dot_t, split(crecv[l]), (wgh[l], wgl[l]))
    near_step(levels)
    b.wait_recv()
    down = three(dot_t, split(crecv[top]), (wgh[top], wgl[top]))
    for l in range(levels - 2, -1, -1):
        down = coup[l] + three(dot_t, split(down), (wth[l], wtl[l]))
    dbuf[p] = down
    d0 = send(dbuf.at[p], dbuf.at[p], far_chip, d_send.at[0], d_recv.at[0])
    d1 = send(dbuf.at[p], dbuf.at[p], core, d_send.at[1], d_recv.at[1])

    for copy in edges:
        copy.wait_recv()
    low = jnp.where(p == 0, 0.0, erecv[0])
    high = jnp.where(p == parts - 1, 0.0, erecv[1])
    ph[:size, :], pl_[:size, :] = split(low)
    ph[size + rows:, :], pl_[size + rows:, :] = split(high)
    d0.wait_recv()
    d2 = send(dbuf.at[p ^ 2], dbuf.at[p ^ 2], core, d_send.at[2], d_recv.at[2])
    near(0, 1)
    near(row_blocks - 1, 1)
    d1.wait_recv()
    d2.wait_recv()
    for q in range(cols // width):
        d_out[q * width:(q + 1) * width, :] = dbuf[q]
    for copy in started + edges + [d0, d1, d2]:
        copy.wait_send()
    for out in outs:
        out.wait()


def tree_call(levels, c, edge, th, tl, ah, al, transfer, coupling):
    cols, rank = c.shape
    rows = th.shape[0]
    row_blocks, size = ah.shape[0], ah.shape[1]
    width = cols // lax.axis_size("pts")
    hbm, vmem = (pl.BlockSpec(memory_space=s) for s in (pl.ANY, pltpu.VMEM))
    shape = jax.ShapeDtypeStruct
    dma = pltpu.SemaphoreType.DMA
    part = (width, rank)
    return pl.pallas_call(
        functools.partial(tree_kernel, levels),
        out_shape=(shape((cols, rank), F32), shape((rows, cols), F32)),
        in_specs=[vmem, vmem, hbm, hbm, hbm, hbm, vmem, vmem],
        out_specs=(vmem, hbm),
        scratch_shapes=[
            pltpu.VMEM((rows + 2 * size, cols), BF16), pltpu.VMEM((rows + 2 * size, cols), BF16),
            pltpu.VMEM(ah.shape, BF16), pltpu.VMEM(al.shape, BF16), pltpu.VMEM((rows, cols), F32),
            pltpu.VMEM(transfer.shape, BF16), pltpu.VMEM(transfer.shape, BF16),
            pltpu.VMEM(coupling.shape, BF16), pltpu.VMEM(coupling.shape, BF16),
            pltpu.VMEM((2,) + part, F32), pltpu.VMEM(part, F32), pltpu.VMEM(part, F32),
            pltpu.VMEM((levels,) + part, F32), pltpu.VMEM((levels - 1,) + part, F32), pltpu.VMEM((levels - 1,) + part, F32),
            pltpu.VMEM((levels,) + part, F32), pltpu.VMEM((levels - 1,) + part, F32),
            pltpu.VMEM((cols // width,) + part, F32), pltpu.VMEM(edge.shape, F32),
            dma((4,)), dma((row_blocks,)), dma((3,)), dma((3,)), dma((levels - 1,)), dma((levels - 1,)),
            dma((levels,)), dma((levels,)), dma((3,)), dma((3,)), dma((2,)), dma((2,)),
        ],
        compiler_params=pltpu.CompilerParams(vmem_limit_bytes=56 * MIB, collective_id=0, has_side_effects=True),
        name="tree_near",
    )(c, edge, th, tl, ah, al, transfer, coupling)


def scatter_kernel(addr, d_in, basis_hbm, near_hbm, out_hbm, bv, nv, ov, rows_f, dh, dl, in_sem, out_sem):
    rows, rank = bv.shape
    cols = nv.shape[1]
    tiles = cols // LANES
    chunk = rows_f.shape[0] // tiles
    chunks = rows // chunk

    def copies(i):
        at = pl.multiple_of(i * chunk, chunk)
        return (pltpu.make_async_copy(basis_hbm.at[pl.ds(at, chunk)], bv.at[pl.ds(at, chunk)], in_sem.at[0, i]),
                pltpu.make_async_copy(near_hbm.at[pl.ds(at, chunk)], nv.at[pl.ds(at, chunk)], in_sem.at[1, i]))

    @pl.loop(0, chunks)
    def _(i):
        for copy in copies(i):
            copy.start()

    for j in range(tiles):
        h, l = split(d_in[j * LANES:(j + 1) * LANES, :].T)
        dh[:, j * LANES:(j + 1) * LANES] = h
        dl[:, j * LANES:(j + 1) * LANES] = l

    @pl.loop(0, chunks)
    def _(i):
        for copy in copies(i):
            copy.wait()
        at = pl.multiple_of(i * chunk, chunk)
        total = nv[pl.ds(at, chunk), :] + three(dot, split(bv[pl.ds(at, chunk), :]), (dh[...], dl[...]))
        for g in range(chunk // SUB):
            for j in range(tiles):
                rows_f[(g * tiles + j) * SUB:(g * tiles + j + 1) * SUB, :] = total[g * SUB:(g + 1) * SUB, j * LANES:(j + 1) * LANES]
        step = 32

        @pl.loop(0, chunk // step)
        def _(g):
            first = i * chunk + g * step
            for u in range(step):
                to = g * (step * tiles) + (u // SUB) * (SUB * tiles) + u % SUB
                ov[pl.ds(addr[first + u], tiles, stride=SUB), :] = rows_f[pl.ds(to, tiles, stride=SUB), :]

    out = pltpu.make_async_copy(ov, out_hbm, out_sem)
    out.start()
    out.wait()


def scatter_call(addr, down, basis, near):
    rows, rank = basis.shape
    cols = near.shape[1]
    tiles = cols // LANES
    chunk = min(256, rows)
    smem, hbm, vmem = (pl.BlockSpec(memory_space=s) for s in (pltpu.SMEM, pl.ANY, pltpu.VMEM))
    return pl.pallas_call(
        scatter_kernel,
        out_shape=jax.ShapeDtypeStruct((rows * tiles, LANES), F32),
        in_specs=[smem, vmem, hbm, hbm],
        out_specs=hbm,
        scratch_shapes=[
            pltpu.VMEM((rows, rank), F32), pltpu.VMEM((rows, cols), F32), pltpu.VMEM((rows * tiles, LANES), F32),
            pltpu.VMEM((chunk * tiles, LANES), F32), pltpu.VMEM((rank, cols), BF16), pltpu.VMEM((rank, cols), BF16),
            pltpu.SemaphoreType.DMA((2, rows // chunk)), pltpu.SemaphoreType.DMA,
        ],
        compiler_params=pltpu.CompilerParams(vmem_limit_bytes=56 * MIB),
        name="far_scatter",
    )(addr, down, basis, near)


def local(points_rhs, order, basis, near_blocks, near_pairs, transfer, coupling):
    rows, cols = points_rhs.shape
    tiles = cols // LANES
    levels = lax.axis_size("leaf").bit_length() - 1
    first = order[0]
    addr = (first // SUB) * (SUB * tiles) + first % SUB
    x = points_rhs.reshape(rows // SUB, SUB, tiles, LANES).transpose(0, 2, 1, 3).reshape(rows * tiles, LANES)
    c, edge, th, tl, ah, al = gather_call(addr, near_pairs.reshape(-1), x, basis, near_blocks)
    down, near = tree_call(levels, c, edge, th, tl, ah, al, transfer[0], coupling[0])
    out = scatter_call(addr, down, basis, near)
    return out.reshape(rows // SUB, tiles, SUB, LANES).transpose(0, 2, 1, 3).reshape(rows, cols)


def solution(mesh):
    return jax.shard_map(
        local,
        mesh=mesh,
        in_specs=(
            P(("leaf", "pts"), None),
            P(("leaf", "pts"), None),
            P(("leaf", "pts"), None),
            P(("leaf", "pts"), None, None),
            P(("leaf", "pts"), None),
            P("leaf", None, None, None),
            P("leaf", None, None, None),
        ),
        out_specs=P(("leaf", "pts"), None),
        check_vma=False,
    )
```

```python
import functools

import jax
import jax.numpy as jnp
from jax import lax
from jax.experimental import pallas as pl
from jax.experimental.pallas import tpu as pltpu
from jax.sharding import PartitionSpec as P

MESH = pl.DeviceIdType.MESH
F32, BF16, I32 = jnp.float32, jnp.bfloat16, jnp.int32
LANES, SUB = 128, 8
MIB = 2**20
CHUNK = 256
HALVES = 2


def split(x):
    hi = x.astype(BF16)
    return hi, (x - hi.astype(F32)).astype(BF16)


def stack(x):
    return jnp.concatenate(split(x), axis=0)


def dot(a, b):
    return jnp.dot(a, b, preferred_element_type=F32)


def dot_t(a, b):
    return lax.dot_general(a, b, (((1,), (1,)), ((), ())), preferred_element_type=F32)


def three(mul, a, bh, bl):
    n = a.shape[0] // 2
    both = mul(a, bh)
    return both[:n] + (both[n:] + mul(a[:n], bl))


def row_address(order, tiles):
    return (order >> 3) * (SUB * tiles) + (order & (SUB - 1))


def tiles_of(ref, tiles, first, count):
    return [
        jnp.concatenate([ref[(g * tiles + j) * SUB:(g * tiles + j + 1) * SUB, :]
                         for g in range(first // SUB, (first + count) // SUB)], axis=0)
        for j in range(tiles)
    ]


def tree_kernel(levels, order_in, pairs_in, x_hbm, basis_hbm, blocks_hbm, t_hbm, g_hbm, d_out, near_hbm,
                xv, bv, bt, rows_a, rows_b, acc, cin, edge, ph, pl_, blk, pre, nv,
                tv, gv, tsib, wt, ws, wf, addr_v, addr, key_v, tab_v, tab,
                rs1, stage, rs2, cb, crecv, own, ebuf, dbuf, erecv,
                in_sem, n_sem, t_send, t_recv, r_send, r_recv, c_send, c_recv, d_send, d_recv, e_send, e_recv):
    rows, cols = nv.shape
    rank = bv.shape[1]
    tiles = cols // LANES
    count, size = blk.shape[0], blk.shape[1]
    row_blocks = rows // size
    width = cin.shape[1]
    half = width // HALVES
    chunks = rows // CHUNK
    leaf, p = lax.axis_index("leaf"), lax.axis_index("pts")
    parts = cin.shape[0]
    top = levels - 1
    core, far_chip = (leaf, p ^ 1), (leaf, p ^ 2)
    following, before = (leaf, lax.rem(p + 1, parts)), (leaf, lax.rem(p + parts - 1, parts))
    siblings = [(leaf ^ (1 << l), p) for l in range(levels)]

    def load(src, dst, i):
        copy = pltpu.make_async_copy(src, dst, in_sem.at[i])
        copy.start()
        return copy

    def send(src, dst, to, send_sem, recv_sem):
        copy = pltpu.make_async_remote_copy(
            src_ref=src, dst_ref=dst, send_sem=send_sem, recv_sem=recv_sem, device_id=to, device_id_type=MESH)
        copy.start()
        return copy

    barrier = pltpu.get_barrier_semaphore()
    greeted = [core, far_chip, (leaf, p ^ 3)] + siblings
    for other in greeted:
        pl.semaphore_signal(barrier, inc=1, device_id=other, device_id_type=MESH)
    in_t = load(t_hbm, tv, 0)
    in_g = load(g_hbm, gv, 1)
    in_b = load(basis_hbm, bv, 2)
    in_x = load(x_hbm, xv, 3)
    in_k = load(blocks_hbm, blk, 4)
    addr_v[...] = row_address(order_in[...], tiles)
    in_a = load(addr_v, addr, 5)

    key_v[...] = jnp.full(key_v.shape, 1e6, F32)
    key_v[0:1, :count] = (2 * pairs_in[0:1, :] + pairs_in[1:2, :]).astype(F32)
    across = jnp.broadcast_to(key_v[0:1, :], (LANES, LANES))
    down_key = across.T
    row_i = lax.broadcasted_iota(I32, (LANES, LANES), 0)
    col_i = lax.broadcasted_iota(I32, (LANES, LANES), 1)
    col_f = col_i.astype(F32)
    one = lambda cond: jnp.where(cond, 1.0, 0.0)
    twin = one((across == down_key) & (col_i < row_i))
    place = jnp.sum(twin + one(across < down_key), axis=1, keepdims=True)
    hit = one(place == col_f)
    again = jnp.where(jnp.sum(twin, axis=1, keepdims=True) > 0, 1.0, 0.0)
    total = lambda x: jnp.sum(x, axis=0, keepdims=True)
    found = total(one(down_key == col_f))
    last = jnp.where(found > 0, total(one(down_key <= col_f)) - 1.0, float(count))
    tab_v[...] = jnp.zeros_like(tab_v)
    tab_v[0:1, :] = total(hit * row_i.astype(F32)).astype(I32)
    tab_v[1:2, :] = total(hit * again).astype(I32)
    tab_v[2:3, :] = last.astype(I32)
    in_tab = load(tab_v, tab, 6)
    pre[0] = jnp.zeros((size, size), F32)
    pre[count] = jnp.zeros((size, size), F32)
    acc[...] = jnp.zeros_like(acc)

    pl.semaphore_wait(barrier, len(greeted))
    moved = [send(t_hbm.at[l], tsib.at[l], siblings[l], t_send.at[l], t_recv.at[l]) for l in range(top)]

    in_t.wait()
    in_g.wait()
    for l in range(top):
        wt[l, 0], wt[l, 1] = split(tv[l])
    wf[...] = tv[0]
    ws[0, 0], ws[0, 1] = split(gv[0])
    for l in range(1, levels):
        path = stack(wf[...])
        gh, gl = split(gv[l])
        ws[l, 0], ws[l, 1] = split(three(dot, path, gh, gl))
        if l < top:
            wf[...] = three(dot, path, wt[l, 0], wt[l, 1])

    in_b.wait()

    @pl.loop(0, chunks)
    def _(i):
        at = pl.multiple_of(i * CHUNK, CHUNK)
        bt[:, pl.ds(at, CHUNK)] = stack(bv[pl.ds(at, CHUNK), :].T)

    in_a.wait()
    in_tab.wait()
    in_x.wait()

    def gather(i, buf):
        step = 32
        for g in range(CHUNK // step):
            ids = [g * step + u for u in range(step)]
            vals = [xv[pl.ds(addr[i * (CHUNK // LANES) + k // LANES, k % LANES], tiles, stride=SUB), :] for k in ids]
            for k, val in zip(ids, vals):
                buf[pl.ds((k // SUB) * (SUB * tiles) + k % SUB, tiles, stride=SUB), :] = val

    def compress(i, buf):
        at = pl.multiple_of(i * CHUNK, CHUNK)
        hi, lo = zip(*[split(part) for part in tiles_of(buf, tiles, 0, CHUNK)])
        hi, lo = jnp.concatenate(hi, axis=1), jnp.concatenate(lo, axis=1)
        to = pl.ds(pl.multiple_of(size + at, size), CHUNK)
        ph[to, :] = hi
        pl_[to, :] = lo
        acc[...] += three(dot, bt[:, pl.ds(at, CHUNK)], hi, lo)

    gather(0, rows_a)
    for j, part in enumerate(tiles_of(rows_a, tiles, 0, size)):
        edge[0, :, j * LANES:(j + 1) * LANES] = part

    @pl.loop(0, chunks // 2 - 1)
    def _(i):
        gather(2 * i + 1, rows_b)
        compress(2 * i, rows_a)
        gather(2 * i + 2, rows_a)
        compress(2 * i + 1, rows_b)

    gather(chunks - 1, rows_b)
    compress(chunks - 2, rows_a)
    for j, part in enumerate(tiles_of(rows_b, tiles, CHUNK - size, size)):
        edge[1, :, j * LANES:(j + 1) * LANES] = part
    compress(chunks - 1, rows_b)
    for q in range(parts):
        cin[q] = acc[:, q * width:(q + 1) * width].T

    hs = [pl.ds(h * half, half) for h in range(HALVES)]
    to_core = [[send(cin.at[p ^ (3 - 2 * k), hs[h]], rs1.at[k, hs[h]], core, r_send.at[k, h], r_recv.at[k, h])
                for h in range(HALVES)] for k in range(2)]
    to_far = []
    for h in range(HALVES):
        to_core[0][h].wait_recv()
        stage[hs[h], :] = cin[p ^ 2, hs[h], :] + rs1[0, hs[h], :]
        to_far.append(send(stage.at[hs[h]], rs2.at[hs[h]], far_chip, r_send.at[2, h], r_recv.at[2, h]))
    for copy in to_core[1]:
        copy.wait_recv()
    sent = to_core[0] + to_core[1] + to_far + moved

    in_k.wait()

    @pl.loop(0, count)
    def _(m):
        pre[m] = jnp.where(tab[1, m] > 0, pre[jnp.maximum(m - 1, 0)], 0.0) + blk[jnp.clip(tab[0, m], 0, count - 1)]

    outs = []

    def near(first, number):
        if not number:
            return

        @pl.loop(first, first + number)
        def _(u):
            none = jnp.zeros((size, size), F32)
            get = lambda r, o: pre[jnp.clip(tab[2, 6 * u + 3 * r + o], 0, count)]
            upper = jnp.concatenate([get(0, 0), get(0, 1), get(0, 2), none], axis=1)
            lower = jnp.concatenate([none, get(1, 0), get(1, 1), get(1, 2)], axis=1)
            band = stack(jnp.concatenate([upper, lower], axis=0))
            at = pl.multiple_of(u * (2 * size), 2 * size)
            span = pl.ds(at, 4 * size)
            nv[pl.ds(at, 2 * size), :] = three(dot, band, ph[span, :], pl_[span, :])

        span = pl.ds(first * 2 * size, number * 2 * size)
        out = pltpu.make_async_copy(nv.at[span], near_hbm.at[span], n_sem.at[first])
        out.start()
        outs.append(out)

    units = row_blocks // 2
    inner = units - 2
    cuts = [1 + inner * i // (levels + 1) for i in range(levels + 2)]

    def near_step(i):
        near(cuts[i], cuts[i + 1] - cuts[i])

    near_step(0)
    for l in range(top):
        moved[l].wait_recv()
        wt[top + l, 0], wt[top + l, 1] = split(tsib[l])

    edges = []
    up = []
    for h in range(HALVES):
        to_far[h].wait_recv()
        cb[0, hs[h], :] = cin[p, hs[h], :] + (rs1[1, hs[h], :] + rs2[hs[h], :])
        up.append(send(cb.at[0, hs[h]], crecv.at[0, hs[h]], siblings[0], c_send.at[0, h], c_recv.at[0, h]))
    for l in range(top):
        if l == 0:
            edges.append(send(edge.at[1], erecv.at[0], following, e_send.at[0], e_recv.at[0]))
            edges.append(send(edge.at[0], erecv.at[1], before, e_send.at[1], e_recv.at[1]))
        own[...] = three(dot, stack(cb[l]), wt[l, 0], wt[l, 1])
        near_step(1 + l)
        for h in range(HALVES):
            up[l * HALVES + h].wait_recv()
            cb[l + 1, hs[h], :] = own[hs[h], :] + three(dot, stack(crecv[l, hs[h], :]), wt[top + l, 0], wt[top + l, 1])
            up.append(send(cb.at[l + 1, hs[h]], crecv.at[l + 1, hs[h]], siblings[l + 1], c_send.at[l + 1, h], c_recv.at[l + 1, h]))
        part = three(dot_t, stack(crecv[l]), ws[l, 0], ws[l, 1])
        ebuf[...] = part if l == 0 else ebuf[...] + part
    near_step(levels)
    d0, d1, d2 = [], [], []
    for h in range(HALVES):
        up[top * HALVES + h].wait_recv()
        dbuf[p, hs[h], :] = ebuf[hs[h], :] + three(dot_t, stack(crecv[top, hs[h], :]), ws[top, 0], ws[top, 1])
        mine = dbuf.at[p, hs[h]]
        d0.append(send(mine, mine, far_chip, d_send.at[0, h], d_recv.at[0, h]))
        d1.append(send(mine, mine, core, d_send.at[1, h], d_recv.at[1, h]))

    for copy in edges:
        copy.wait_recv()
    ph[:size, :], pl_[:size, :] = split(jnp.where(p == 0, 0.0, erecv[0]))
    ph[size + rows:, :], pl_[size + rows:, :] = split(jnp.where(p == parts - 1, 0.0, erecv[1]))
    near(0, 1)
    near(units - 1, 1)
    for h in range(HALVES):
        d0[h].wait_recv()
        other = dbuf.at[p ^ 2, hs[h]]
        d2.append(send(other, other, core, d_send.at[2, h], d_recv.at[2, h]))
    for copy in d1 + d2:
        copy.wait_recv()
    for q in range(parts):
        d_out[q * width:(q + 1) * width, :] = dbuf[q]
    for copy in sent + up + edges + d0 + d1 + d2:
        copy.wait_send()
    for out in outs:
        out.wait()


def tree_call(levels, parts, order, pairs, x, basis, blocks, transfer, coupling):
    rows, rank = basis.shape
    tiles = x.shape[0] // rows
    cols = tiles * LANES
    count, size = blocks.shape[0], blocks.shape[1]
    width = cols // parts
    hbm, vmem = (pl.BlockSpec(memory_space=s) for s in (pl.ANY, pltpu.VMEM))
    shape = jax.ShapeDtypeStruct
    dma = pltpu.SemaphoreType.DMA
    part = (width, rank)
    padded = (rows + 2 * size, cols)
    scratch = [
        (x.shape, F32), (basis.shape, F32), ((2 * rank, rows), BF16), ((CHUNK * tiles, LANES), F32), ((CHUNK * tiles, LANES), F32),
        ((rank, cols), F32), ((parts,) + part, F32), ((2, size, cols), F32), (padded, BF16), (padded, BF16),
        (blocks.shape, F32), ((count + 1, size, size), F32), ((rows, cols), F32),
        (transfer.shape, F32), (coupling.shape, F32), (transfer.shape, F32),
        ((2 * (levels - 1), 2, rank, rank), BF16), ((levels, 2, rank, rank), BF16), ((rank, rank), F32),
        (order.shape, I32), None, ((SUB, LANES), F32), ((SUB, LANES), I32), None,
        ((2,) + part, F32), (part, F32), (part, F32), ((levels,) + part, F32), ((levels,) + part, F32),
        (part, F32), (part, F32), ((parts,) + part, F32), ((2, size, cols), F32),
    ]
    scratch = [pltpu.VMEM(*s) if s else None for s in scratch]
    scratch[20] = pltpu.SMEM(order.shape, I32)
    scratch[23] = pltpu.SMEM((SUB, LANES), I32)
    return pl.pallas_call(
        functools.partial(tree_kernel, levels),
        out_shape=(shape((cols, rank), F32), shape((rows, cols), F32)),
        in_specs=[vmem, vmem, hbm, hbm, hbm, hbm, hbm],
        out_specs=(vmem, hbm),
        scratch_shapes=scratch + [
            dma((7,)), dma((rows // size,)), dma((levels - 1,)), dma((levels - 1,)), dma((3, HALVES)), dma((3, HALVES)),
            dma((levels, HALVES)), dma((levels, HALVES)), dma((3, HALVES)), dma((3, HALVES)), dma((2,)), dma((2,)),
        ],
        compiler_params=pltpu.CompilerParams(vmem_limit_bytes=60 * MIB, collective_id=0, has_side_effects=True),
        name="tree_near",
    )(order, pairs, x, basis, blocks, transfer, coupling)


def scatter_kernel(order_in, d_in, basis_hbm, near_hbm, out_hbm, bv, nv, ov, rows_a, rows_b, dh, dl, addr_v, addr, in_sem, a_sem, out_sem):
    rows, rank = bv.shape
    cols = nv.shape[1]
    tiles = cols // LANES
    chunks = rows // CHUNK

    def copies(i):
        at = pl.multiple_of(i * CHUNK, CHUNK)
        return (pltpu.make_async_copy(basis_hbm.at[pl.ds(at, CHUNK)], bv.at[pl.ds(at, CHUNK)], in_sem.at[0, i]),
                pltpu.make_async_copy(near_hbm.at[pl.ds(at, CHUNK)], nv.at[pl.ds(at, CHUNK)], in_sem.at[1, i]))

    @pl.loop(0, chunks)
    def _(i):
        for copy in copies(i):
            copy.start()

    addr_v[...] = row_address(order_in[...], tiles)
    in_a = pltpu.make_async_copy(addr_v, addr, a_sem)
    in_a.start()
    for j in range(tiles):
        h, l = split(d_in[j * LANES:(j + 1) * LANES, :].T)
        dh[:, j * LANES:(j + 1) * LANES] = h
        dl[:, j * LANES:(j + 1) * LANES] = l
    in_a.wait()

    def wait(i):
        for copy in copies(i):
            copy.wait()

    def multiply(i, buf):
        at = pl.multiple_of(i * CHUNK, CHUNK)
        total = nv[pl.ds(at, CHUNK), :] + three(dot, stack(bv[pl.ds(at, CHUNK), :]), dh[...], dl[...])
        for g in range(CHUNK // SUB):
            for j in range(tiles):
                buf[(g * tiles + j) * SUB:(g * tiles + j + 1) * SUB, :] = total[g * SUB:(g + 1) * SUB, j * LANES:(j + 1) * LANES]

    def scatter(i, buf):
        for k in range(CHUNK):
            to = addr[i * (CHUNK // LANES) + k // LANES, k % LANES]
            ov[pl.ds(to, tiles, stride=SUB), :] = buf[pl.ds((k // SUB) * (SUB * tiles) + k % SUB, tiles, stride=SUB), :]

    wait(0)
    multiply(0, rows_a)

    @pl.loop(0, chunks // 2 - 1)
    def _(i):
        wait(2 * i + 1)
        multiply(2 * i + 1, rows_b)
        scatter(2 * i, rows_a)
        wait(2 * i + 2)
        multiply(2 * i + 2, rows_a)
        scatter(2 * i + 1, rows_b)

    wait(chunks - 1)
    multiply(chunks - 1, rows_b)
    scatter(chunks - 2, rows_a)
    scatter(chunks - 1, rows_b)
    out = pltpu.make_async_copy(ov, out_hbm, out_sem)
    out.start()
    out.wait()


def scatter_call(order, down, basis, near):
    rows, rank = basis.shape
    cols = near.shape[1]
    tiles = cols // LANES
    hbm, vmem = (pl.BlockSpec(memory_space=s) for s in (pl.ANY, pltpu.VMEM))
    return pl.pallas_call(
        scatter_kernel,
        out_shape=jax.ShapeDtypeStruct((rows * tiles, LANES), F32),
        in_specs=[vmem, vmem, hbm, hbm],
        out_specs=hbm,
        scratch_shapes=[
            pltpu.VMEM((rows, rank), F32), pltpu.VMEM((rows, cols), F32), pltpu.VMEM((rows * tiles, LANES), F32),
            pltpu.VMEM((CHUNK * tiles, LANES), F32), pltpu.VMEM((CHUNK * tiles, LANES), F32),
            pltpu.VMEM((rank, cols), BF16), pltpu.VMEM((rank, cols), BF16),
            pltpu.VMEM(order.shape, I32), pltpu.SMEM(order.shape, I32),
            pltpu.SemaphoreType.DMA((2, rows // CHUNK)), pltpu.SemaphoreType.DMA, pltpu.SemaphoreType.DMA,
        ],
        compiler_params=pltpu.CompilerParams(vmem_limit_bytes=56 * MIB),
        name="far_scatter",
    )(order, down, basis, near)


def local(points_rhs, order, basis, near_blocks, near_pairs, transfer, coupling):
    rows, cols = points_rhs.shape
    tiles = cols // LANES
    levels = lax.axis_size("leaf").bit_length() - 1
    order = order.reshape(rows // LANES, LANES)
    x = points_rhs.reshape(rows // SUB, SUB, tiles, LANES).transpose(0, 2, 1, 3).reshape(rows * tiles, LANES)
    down, near = tree_call(levels, lax.axis_size("pts"), order, near_pairs.T, x, basis, near_blocks, transfer[0], coupling[0])
    out = scatter_call(order, down, basis, near)
    return out.reshape(rows // SUB, tiles, SUB, LANES).transpose(0, 2, 1, 3).reshape(rows, cols)


def solution(mesh):
    return jax.shard_map(
        local,
        mesh=mesh,
        in_specs=(
            P(("leaf", "pts"), None),
            P(("leaf", "pts"), None),
            P(("leaf", "pts"), None),
            P(("leaf", "pts"), None, None),
            P(("leaf", "pts"), None),
            P("leaf", None, None, None),
            P("leaf", None, None, None),
        ),
        out_specs=P(("leaf", "pts"), None),
        check_vma=False,
    )
```

```python
import functools

import jax
import jax.numpy as jnp
from jax import lax
from jax.experimental import pallas as pl
from jax.experimental.pallas import tpu as pltpu
from jax.sharding import PartitionSpec as P

MESH = pl.DeviceIdType.MESH
F32, BF16, I32 = jnp.float32, jnp.bfloat16, jnp.int32
LANES, SUB = 128, 8
MIB = 2**20
CHUNK = 256
HALVES = 2


def split(x):
    hi = x.astype(BF16)
    return hi, (x - hi.astype(F32)).astype(BF16)


def stack(x):
    return jnp.concatenate(split(x), axis=0)


def dot(a, b):
    return jnp.dot(a, b, preferred_element_type=F32)


def dot_t(a, b):
    return lax.dot_general(a, b, (((1,), (1,)), ((), ())), preferred_element_type=F32)


def three(mul, a, bh, bl):
    n = a.shape[0] // 2
    both = mul(a, bh)
    return both[:n] + (both[n:] + mul(a[:n], bl))


def row_address(order, tiles):
    return (order >> 3) * (SUB * tiles) + (order & (SUB - 1))


def tiles_of(ref, tiles, first, count):
    return [
        jnp.concatenate([ref[(g * tiles + j) * SUB:(g * tiles + j + 1) * SUB, :]
                         for g in range(first // SUB, (first + count) // SUB)], axis=0)
        for j in range(tiles)
    ]


def tree_kernel(levels, order_in, pairs_in, x_hbm, basis_hbm, blocks_hbm, t_hbm, g_hbm, d_out, nv, split_out,
                xv, bv, bt, rows_a, rows_b, acc, cin, edge, ph, pl_, blk, pre,
                tv, gv, tsib, wt, ws, wf, addr_v, addr, key_v, tab_v, tab,
                rs1, stage, rs2, cb, crecv, own, ebuf, dbuf, erecv,
                in_sem, t_send, t_recv, r_send, r_recv, c_send, c_recv, d_send, d_recv, e_send, e_recv):
    rows, cols = nv.shape
    rank = bv.shape[1]
    tiles = cols // LANES
    count, size = blk.shape[0], blk.shape[1]
    row_blocks = rows // size
    parts, half = cin.shape[1:3]
    chunks = rows // CHUNK
    leaf, p = lax.axis_index("leaf"), lax.axis_index("pts")
    top = levels - 1
    core, far_chip = (leaf, p ^ 1), (leaf, p ^ 2)
    following, before = (leaf, lax.rem(p + 1, parts)), (leaf, lax.rem(p + parts - 1, parts))
    siblings = [(leaf ^ (1 << l), p) for l in range(levels)]

    def load(src, dst, i):
        copy = pltpu.make_async_copy(src, dst, in_sem.at[i])
        copy.start()
        return copy

    def send(src, dst, to, send_sem, recv_sem):
        copy = pltpu.make_async_remote_copy(
            src_ref=src, dst_ref=dst, send_sem=send_sem, recv_sem=recv_sem, device_id=to, device_id_type=MESH)
        copy.start()
        return copy

    barrier = pltpu.get_barrier_semaphore()
    greeted = [core, far_chip, (leaf, p ^ 3)] + siblings
    for other in greeted:
        pl.semaphore_signal(barrier, inc=1, device_id=other, device_id_type=MESH)
    addr_v[...] = row_address(order_in[...], tiles)
    in_a = load(addr_v, addr, 5)
    in_x = load(x_hbm, xv, 3)
    in_b = load(basis_hbm, bv, 2)
    in_t = load(t_hbm, tv, 0)
    in_g = load(g_hbm, gv, 1)
    in_k = load(blocks_hbm, blk, 4)

    key_v[...] = jnp.full(key_v.shape, 1e6, F32)
    key_v[0:1, :count] = (2 * pairs_in[0:1, :] + pairs_in[1:2, :]).astype(F32)
    across = jnp.broadcast_to(key_v[0:1, :], (LANES, LANES))
    down_key = across.T
    row_i = lax.broadcasted_iota(I32, (LANES, LANES), 0)
    col_i = lax.broadcasted_iota(I32, (LANES, LANES), 1)
    col_f = col_i.astype(F32)
    one = lambda cond: jnp.where(cond, 1.0, 0.0)
    twin = one((across == down_key) & (col_i < row_i))
    place = jnp.sum(twin + one(across < down_key), axis=1, keepdims=True)
    hit = one(place == col_f)
    again = jnp.where(jnp.sum(twin, axis=1, keepdims=True) > 0, 1.0, 0.0)
    total = lambda x: jnp.sum(x, axis=0, keepdims=True)
    found = total(one(down_key == col_f))
    last = jnp.where(found > 0, total(one(down_key <= col_f)) - 1.0, float(count))
    tab_v[...] = jnp.zeros_like(tab_v)
    tab_v[0:1, :] = total(hit * row_i.astype(F32)).astype(I32)
    tab_v[1:2, :] = total(hit * again).astype(I32)
    tab_v[2:3, :] = last.astype(I32)
    in_tab = load(tab_v, tab, 6)
    pre[0] = jnp.zeros((size, size), F32)
    pre[count] = jnp.zeros((size, size), F32)
    in_a.wait()
    in_tab.wait()
    in_x.wait()

    def gather(i, buf):
        step = 32
        for g in range(CHUNK // step):
            ids = [g * step + u for u in range(step)]
            vals = [xv[pl.ds(addr[i * (CHUNK // LANES) + k // LANES, k % LANES], tiles, stride=SUB), :] for k in ids]
            for k, val in zip(ids, vals):
                buf[pl.ds((k // SUB) * (SUB * tiles) + k % SUB, tiles, stride=SUB), :] = val

    def keep(i, buf):
        to = pl.ds(pl.multiple_of(size + i * CHUNK, size), CHUNK)
        for j, part in enumerate(tiles_of(buf, tiles, 0, CHUNK)):
            ph[to, j * LANES:(j + 1) * LANES], pl_[to, j * LANES:(j + 1) * LANES] = split(part)

    gather(0, rows_a)
    pl.semaphore_wait(barrier, len(greeted))
    moved = [send(t_hbm.at[l], tsib.at[l], siblings[l], t_send.at[l], t_recv.at[l]) for l in range(top)]
    for j, part in enumerate(tiles_of(rows_a, tiles, 0, size)):
        edge[0, :, j * LANES:(j + 1) * LANES] = part

    @pl.loop(0, chunks // 2 - 1)
    def _(i):
        gather(2 * i + 1, rows_b)
        keep(2 * i, rows_a)
        gather(2 * i + 2, rows_a)
        keep(2 * i + 1, rows_b)

    gather(chunks - 1, rows_b)
    keep(chunks - 2, rows_a)
    for j, part in enumerate(tiles_of(rows_b, tiles, CHUNK - size, size)):
        edge[1, :, j * LANES:(j + 1) * LANES] = part
    keep(chunks - 1, rows_b)
    in_b.wait()

    @pl.loop(0, chunks)
    def _(i):
        at = pl.multiple_of(i * CHUNK, CHUNK)
        bt[:, pl.ds(at, CHUNK)] = stack(bv[pl.ds(at, CHUNK), :].T)

    span = cols // HALVES

    def compress(h, first, last):
        deep = min(1024, rows)

        @pl.loop(first * rows // deep // 2, last * rows // deep // 2)
        def _(i):
            at = pl.multiple_of(i * deep, deep)
            to = pl.ds(pl.multiple_of(size + at, size), deep)
            part = three(dot, bt[:, pl.ds(at, deep)], ph[to, h * span:(h + 1) * span], pl_[to, h * span:(h + 1) * span])
            acc[...] = jnp.where(i == 0, part, acc[...] + part)

        if last == 2:
            for q in range(span // LANES):
                turned = acc[:, q * LANES:(q + 1) * LANES].T
                for k in range(LANES // half):
                    cin[h, q * (LANES // half) + k] = turned[k * half:(k + 1) * half]

    hs = [pl.ds(h * half, half) for h in range(HALVES)]
    to_core = [[], []]
    to_far = []

    def sum_core(h):
        for k in range(2):
            to_core[k].append(send(cin.at[h, p ^ (3 - 2 * k)], rs1.at[k, hs[h]], core, r_send.at[k, h], r_recv.at[k, h]))

    def sum_far(h):
        to_core[0][h].wait_recv()
        stage[hs[h], :] = cin[h, p ^ 2] + rs1[0, hs[h], :]
        to_far.append(send(stage.at[hs[h]], rs2.at[hs[h]], far_chip, r_send.at[2, h], r_recv.at[2, h]))

    acc[...] = jnp.zeros_like(acc)
    compress(0, 0, 2)
    sum_core(0)
    for h in range(1, HALVES):
        compress(h, 0, 1)
        sum_far(h - 1)
        compress(h, 1, 2)
        sum_core(h)
    sum_far(HALVES - 1)
    for copy in to_core[1]:
        copy.wait_recv()
    sent = to_core[0] + to_core[1] + to_far + moved

    in_t.wait()
    in_g.wait()
    for l in range(top):
        wt[l, 0], wt[l, 1] = split(tv[l])
    wf[...] = tv[0]
    ws[0, 0], ws[0, 1] = split(gv[0])
    for l in range(1, levels):
        path = stack(wf[...])
        gh, gl = split(gv[l])
        ws[l, 0], ws[l, 1] = split(three(dot, path, gh, gl))
        if l < top:
            wf[...] = three(dot, path, wt[l, 0], wt[l, 1])

    in_k.wait()

    @pl.loop(0, count)
    def _(m):
        pre[m] = jnp.where(tab[1, m] > 0, pre[jnp.maximum(m - 1, 0)], 0.0) + blk[jnp.clip(tab[0, m], 0, count - 1)]

    def near(first, number):
        if not number:
            return

        @pl.loop(first, first + number)
        def _(u):
            none = jnp.zeros((size, size), F32)
            get = lambda r, o: pre[jnp.clip(tab[2, 6 * u + 3 * r + o], 0, count)]
            upper = jnp.concatenate([get(0, 0), get(0, 1), get(0, 2), none], axis=1)
            lower = jnp.concatenate([none, get(1, 0), get(1, 1), get(1, 2)], axis=1)
            band = stack(jnp.concatenate([upper, lower], axis=0))
            at = pl.multiple_of(u * (2 * size), 2 * size)
            span = pl.ds(at, 4 * size)
            nv[pl.ds(at, 2 * size), :] = three(dot, band, ph[span, :], pl_[span, :])

    units = row_blocks // 2
    inner = units - 2
    cuts = [1 + inner * i // (levels + 1) for i in range(levels + 2)]

    def near_step(i):
        near(cuts[i], cuts[i + 1] - cuts[i])

    near_step(0)
    for l in range(top):
        moved[l].wait_recv()
        wt[top + l, 0], wt[top + l, 1] = split(tsib[l])

    edges = []
    up = []
    for h in range(HALVES):
        to_far[h].wait_recv()
        cb[0, hs[h], :] = cin[h, p] + (rs1[1, hs[h], :] + rs2[hs[h], :])
        up.append(send(cb.at[0, hs[h]], crecv.at[0, hs[h]], siblings[0], c_send.at[0, h], c_recv.at[0, h]))
    for l in range(top):
        if l == 0:
            edges.append(send(edge.at[1], erecv.at[0], following, e_send.at[0], e_recv.at[0]))
            edges.append(send(edge.at[0], erecv.at[1], before, e_send.at[1], e_recv.at[1]))
        own[...] = three(dot, stack(cb[l]), wt[l, 0], wt[l, 1])
        near_step(1 + l)
        for h in range(HALVES):
            up[l * HALVES + h].wait_recv()
            cb[l + 1, hs[h], :] = own[hs[h], :] + three(dot, stack(crecv[l, hs[h], :]), wt[top + l, 0], wt[top + l, 1])
            up.append(send(cb.at[l + 1, hs[h]], crecv.at[l + 1, hs[h]], siblings[l + 1], c_send.at[l + 1, h], c_recv.at[l + 1, h]))
        part = three(dot_t, stack(crecv[l]), ws[l, 0], ws[l, 1])
        ebuf[...] = part if l == 0 else ebuf[...] + part
    near_step(levels)

    @pl.loop(0, chunks)
    def _(i):
        at = pl.multiple_of(i * CHUNK, CHUNK)
        split_out[pl.ds(2 * at, 2 * CHUNK), :] = stack(bv[pl.ds(at, CHUNK), :])

    d0, d1, d2 = [], [], []
    for h in range(HALVES):
        up[top * HALVES + h].wait_recv()
        dbuf[h, p] = ebuf[hs[h], :] + three(dot_t, stack(crecv[top, hs[h], :]), ws[top, 0], ws[top, 1])
        mine = dbuf.at[h, p]
        d0.append(send(mine, mine, far_chip, d_send.at[0, h], d_recv.at[0, h]))
        d1.append(send(mine, mine, core, d_send.at[1, h], d_recv.at[1, h]))

    for copy in edges:
        copy.wait_recv()
    ph[:size, :], pl_[:size, :] = split(jnp.where(p == 0, 0.0, erecv[0]))
    ph[size + rows:, :], pl_[size + rows:, :] = split(jnp.where(p == parts - 1, 0.0, erecv[1]))
    near(0, 1)
    near(units - 1, 1)
    for h in range(HALVES):
        d0[h].wait_recv()
        other = dbuf.at[h, p ^ 2]
        d2.append(send(other, other, core, d_send.at[2, h], d_recv.at[2, h]))
    for copy in d1 + d2:
        copy.wait_recv()
    for h in range(HALVES):
        for q in range(parts):
            at = (h * parts + q) * half
            d_out[at:at + half, :] = dbuf[h, q]
    for copy in sent + up + edges + d0 + d1 + d2:
        copy.wait_send()


def tree_call(levels, parts, order, pairs, x, basis, blocks, transfer, coupling):
    rows, rank = basis.shape
    tiles = x.shape[0] // rows
    cols = tiles * LANES
    count, size = blocks.shape[0], blocks.shape[1]
    width = cols // parts
    hbm, vmem = (pl.BlockSpec(memory_space=s) for s in (pl.ANY, pltpu.VMEM))
    shape = jax.ShapeDtypeStruct
    dma = pltpu.SemaphoreType.DMA
    part = (width, rank)
    by_half = (HALVES, parts, width // HALVES, rank)
    padded = (rows + 2 * size, cols)
    scratch = [
        (x.shape, F32), (basis.shape, F32), ((2 * rank, rows), BF16), ((CHUNK * tiles, LANES), F32), ((CHUNK * tiles, LANES), F32),
        ((rank, cols // HALVES), F32), (by_half, F32), ((2, size, cols), F32), (padded, BF16), (padded, BF16),
        (blocks.shape, F32), ((count + 1, size, size), F32),
        (transfer.shape, F32), (coupling.shape, F32), (transfer.shape, F32),
        ((2 * (levels - 1), 2, rank, rank), BF16), ((levels, 2, rank, rank), BF16), ((rank, rank), F32),
        (order.shape, I32), None, ((SUB, LANES), F32), ((SUB, LANES), I32), None,
        ((2,) + part, F32), (part, F32), (part, F32), ((levels,) + part, F32), ((levels,) + part, F32),
        (part, F32), (part, F32), (by_half, F32), ((2, size, cols), F32),
    ]
    scratch = [pltpu.VMEM(*s) if s else None for s in scratch]
    scratch[19] = pltpu.SMEM(order.shape, I32)
    scratch[22] = pltpu.SMEM((SUB, LANES), I32)
    return pl.pallas_call(
        functools.partial(tree_kernel, levels),
        out_shape=(pltpu.VMEM((cols, rank), F32), pltpu.VMEM((rows, cols), F32), pltpu.VMEM((2 * rows, rank), BF16)),
        in_specs=[vmem, vmem, hbm, hbm, hbm, hbm, hbm],
        out_specs=(vmem, vmem, vmem),
        scratch_shapes=scratch + [
            dma((7,)), dma((levels - 1,)), dma((levels - 1,)), dma((3, HALVES)), dma((3, HALVES)),
            dma((levels, HALVES)), dma((levels, HALVES)), dma((3, HALVES)), dma((3, HALVES)), dma((2,)), dma((2,)),
        ],
        compiler_params=pltpu.CompilerParams(vmem_limit_bytes=48 * MIB, collective_id=0, has_side_effects=True),
        name="tree_near",
    )(order, pairs, x, basis, blocks, transfer, coupling)


def scatter_kernel(order_in, d_in, basis, near, out_hbm, ov, rows_a, rows_b, dh, dl, addr_v, addr, a_sem, out_sem):
    rows, cols = near.shape
    tiles = cols // LANES
    chunks = rows // CHUNK
    addr_v[...] = row_address(order_in[...], tiles)
    in_a = pltpu.make_async_copy(addr_v, addr, a_sem)
    in_a.start()
    for j in range(tiles):
        h, l = split(d_in[j * LANES:(j + 1) * LANES, :].T)
        dh[:, j * LANES:(j + 1) * LANES] = h
        dl[:, j * LANES:(j + 1) * LANES] = l
    in_a.wait()

    def multiply(i, buf):
        at = pl.multiple_of(i * CHUNK, CHUNK)
        total = near[pl.ds(at, CHUNK), :] + three(dot, basis[pl.ds(2 * at, 2 * CHUNK), :], dh[...], dl[...])
        for g in range(CHUNK // SUB):
            for j in range(tiles):
                buf[(g * tiles + j) * SUB:(g * tiles + j + 1) * SUB, :] = total[g * SUB:(g + 1) * SUB, j * LANES:(j + 1) * LANES]

    def scatter(i, buf):
        for k in range(CHUNK):
            to = addr[i * (CHUNK // LANES) + k // LANES, k % LANES]
            ov[pl.ds(to, tiles, stride=SUB), :] = buf[pl.ds((k // SUB) * (SUB * tiles) + k % SUB, tiles, stride=SUB), :]

    multiply(0, rows_a)

    @pl.loop(0, chunks // 2 - 1)
    def _(i):
        multiply(2 * i + 1, rows_b)
        scatter(2 * i, rows_a)
        multiply(2 * i + 2, rows_a)
        scatter(2 * i + 1, rows_b)

    multiply(chunks - 1, rows_b)
    scatter(chunks - 2, rows_a)
    scatter(chunks - 1, rows_b)
    out = pltpu.make_async_copy(ov, out_hbm, out_sem)
    out.start()
    out.wait()


def scatter_call(order, down, basis, near):
    rows, cols = near.shape
    rank = basis.shape[1]
    tiles = cols // LANES
    hbm, vmem = (pl.BlockSpec(memory_space=s) for s in (pl.ANY, pltpu.VMEM))
    return pl.pallas_call(
        scatter_kernel,
        out_shape=jax.ShapeDtypeStruct((rows * tiles, LANES), F32),
        in_specs=[vmem, vmem, vmem, vmem],
        out_specs=hbm,
        scratch_shapes=[
            pltpu.VMEM((rows * tiles, LANES), F32),
            pltpu.VMEM((CHUNK * tiles, LANES), F32), pltpu.VMEM((CHUNK * tiles, LANES), F32),
            pltpu.VMEM((rank, cols), BF16), pltpu.VMEM((rank, cols), BF16),
            pltpu.VMEM(order.shape, I32), pltpu.SMEM(order.shape, I32),
            pltpu.SemaphoreType.DMA, pltpu.SemaphoreType.DMA,
        ],
        compiler_params=pltpu.CompilerParams(vmem_limit_bytes=24 * MIB),
        name="far_scatter",
    )(order, down, basis, near)


def local(points_rhs, order, basis, near_blocks, near_pairs, transfer, coupling):
    rows, cols = points_rhs.shape
    tiles = cols // LANES
    levels = lax.axis_size("leaf").bit_length() - 1
    order = order.reshape(rows // LANES, LANES)
    x = points_rhs.reshape(rows // SUB, SUB, tiles, LANES).transpose(0, 2, 1, 3).reshape(rows * tiles, LANES)
    down, near, halves = tree_call(levels, lax.axis_size("pts"), order, near_pairs.T, x, basis, near_blocks, transfer[0], coupling[0])
    out = scatter_call(order, *(pltpu.with_memory_space_constraint(v, pltpu.VMEM) for v in (down, halves, near)))
    return out.reshape(rows // SUB, tiles, SUB, LANES).transpose(0, 2, 1, 3).reshape(rows, cols)


def solution(mesh):
    return jax.shard_map(
        local,
        mesh=mesh,
        in_specs=(
            P(("leaf", "pts"), None),
            P(("leaf", "pts"), None),
            P(("leaf", "pts"), None),
            P(("leaf", "pts"), None, None),
            P(("leaf", "pts"), None),
            P("leaf", None, None, None),
            P("leaf", None, None, None),
        ),
        out_specs=P(("leaf", "pts"), None),
        check_vma=False,
    )
```

```python
import functools

import jax
import jax.numpy as jnp
from jax import lax
from jax.experimental import pallas as pl
from jax.experimental.pallas import tpu as pltpu
from jax.sharding import PartitionSpec as P

MESH = pl.DeviceIdType.MESH
F32, BF16, I32 = jnp.float32, jnp.bfloat16, jnp.int32
LANES, SUB = 128, 8
MIB = 2**20
CHUNK = 256
PIECES = 4


def split(x):
    hi = x.astype(BF16)
    return hi, (x - hi.astype(F32)).astype(BF16)


def stack(x):
    return jnp.concatenate(split(x), axis=0)


def dot(a, b):
    return jnp.dot(a, b, preferred_element_type=F32)


def dot_t(a, b):
    return lax.dot_general(a, b, (((1,), (1,)), ((), ())), preferred_element_type=F32)


def three(mul, a, bh, bl):
    n = a.shape[0] // 2
    both = mul(a, bh)
    return both[:n] + (both[n:] + mul(a[:n], bl))


def row_address(order, tiles):
    return (order >> 3) * (SUB * tiles) + (order & (SUB - 1))


def tiles_of(ref, tiles, first, count):
    return [
        jnp.concatenate([ref[(g * tiles + j) * SUB:(g * tiles + j + 1) * SUB, :]
                         for g in range(first // SUB, (first + count) // SUB)], axis=0)
        for j in range(tiles)
    ]


def tree_kernel(levels, order_in, pairs_in, x_hbm, basis_hbm, blocks_hbm, t_hbm, g_hbm, d_out, nv, split_out,
                xv, bv, bt, rows_a, rows_b, acc, cin, edge, ph, pl_, blk, pre,
                tv, gv, tsib, wt, ws, wf, addr_v, addr, key_v, tab_v, tab,
                rs1, stage, rs2, cb, crecv, own, ebuf, dbuf, erecv,
                in_sem, t_send, t_recv, r_send, r_recv, c_send, c_recv, d_send, d_recv, e_send, e_recv):
    rows, cols = nv.shape
    rank = bv.shape[1]
    tiles = cols // LANES
    count, size = blk.shape[0], blk.shape[1]
    row_blocks = rows // size
    parts, width = cin.shape[:2]
    piece = width // PIECES
    chunks = rows // CHUNK
    leaf, p = lax.axis_index("leaf"), lax.axis_index("pts")
    top = levels - 1
    core, far_chip = (leaf, p ^ 1), (leaf, p ^ 2)
    following, before = (leaf, lax.rem(p + 1, parts)), (leaf, lax.rem(p + parts - 1, parts))
    siblings = [(leaf ^ (1 << l), p) for l in range(levels)]

    def load(src, dst, i):
        copy = pltpu.make_async_copy(src, dst, in_sem.at[i])
        copy.start()
        return copy

    def send(src, dst, to, send_sem, recv_sem):
        copy = pltpu.make_async_remote_copy(
            src_ref=src, dst_ref=dst, send_sem=send_sem, recv_sem=recv_sem, device_id=to, device_id_type=MESH)
        copy.start()
        return copy

    barrier = pltpu.get_barrier_semaphore()
    greeted = [core, far_chip, (leaf, p ^ 3)] + siblings
    for other in greeted:
        pl.semaphore_signal(barrier, inc=1, device_id=other, device_id_type=MESH)
    addr_v[...] = row_address(order_in[...], tiles)
    in_a = load(addr_v, addr, 5)
    in_b = load(basis_hbm, bv, 2)
    in_x = load(x_hbm, xv, 3)
    in_t = load(t_hbm, tv, 0)
    in_g = load(g_hbm, gv, 1)
    in_k = load(blocks_hbm, blk, 4)

    key_v[...] = jnp.full(key_v.shape, 1e6, F32)
    key_v[0:1, :count] = (2 * pairs_in[0:1, :] + pairs_in[1:2, :]).astype(F32)
    across = jnp.broadcast_to(key_v[0:1, :], (LANES, LANES))
    down_key = across.T
    row_i = lax.broadcasted_iota(I32, (LANES, LANES), 0)
    col_i = lax.broadcasted_iota(I32, (LANES, LANES), 1)
    col_f = col_i.astype(F32)
    one = lambda cond: jnp.where(cond, 1.0, 0.0)
    twin = one((across == down_key) & (col_i < row_i))
    place = jnp.sum(twin + one(across < down_key), axis=1, keepdims=True)
    hit = one(place == col_f)
    again = jnp.where(jnp.sum(twin, axis=1, keepdims=True) > 0, 1.0, 0.0)
    total = lambda x: jnp.sum(x, axis=0, keepdims=True)
    found = total(one(down_key == col_f))
    last = jnp.where(found > 0, total(one(down_key <= col_f)) - 1.0, float(count))
    tab_v[...] = jnp.zeros_like(tab_v)
    tab_v[0:1, :] = total(hit * row_i.astype(F32)).astype(I32)
    tab_v[1:2, :] = total(hit * again).astype(I32)
    tab_v[2:3, :] = last.astype(I32)
    in_tab = load(tab_v, tab, 6)
    pre[0] = jnp.zeros((size, size), F32)
    pre[count] = jnp.zeros((size, size), F32)
    acc[...] = jnp.zeros_like(acc)
    in_b.wait()

    @pl.loop(0, chunks)
    def _(i):
        at = pl.multiple_of(i * CHUNK, CHUNK)
        bt[:, pl.ds(at, CHUNK)] = stack(bv[pl.ds(at, CHUNK), :].T)

    in_a.wait()
    in_tab.wait()
    in_x.wait()

    def gather(i, buf):
        step = 32
        for g in range(CHUNK // step):
            ids = [g * step + u for u in range(step)]
            vals = [xv[pl.ds(addr[i * (CHUNK // LANES) + k // LANES, k % LANES], tiles, stride=SUB), :] for k in ids]
            for k, val in zip(ids, vals):
                buf[pl.ds((k // SUB) * (SUB * tiles) + k % SUB, tiles, stride=SUB), :] = val

    def compress(i, buf):
        at = pl.multiple_of(i * CHUNK, CHUNK)
        hi, lo = zip(*[split(part) for part in tiles_of(buf, tiles, 0, CHUNK)])
        hi, lo = jnp.concatenate(hi, axis=1), jnp.concatenate(lo, axis=1)
        to = pl.ds(pl.multiple_of(size + at, size), CHUNK)
        ph[to, :] = hi
        pl_[to, :] = lo
        acc[...] += three(dot, bt[:, pl.ds(at, CHUNK)], hi, lo)

    gather(0, rows_a)
    pl.semaphore_wait(barrier, len(greeted))
    moved = [send(t_hbm.at[l], tsib.at[l], siblings[l], t_send.at[l], t_recv.at[l]) for l in range(top)]
    for j, part in enumerate(tiles_of(rows_a, tiles, 0, size)):
        edge[0, :, j * LANES:(j + 1) * LANES] = part

    @pl.loop(0, chunks // 2 - 1)
    def _(i):
        gather(2 * i + 1, rows_b)
        compress(2 * i, rows_a)
        gather(2 * i + 2, rows_a)
        compress(2 * i + 1, rows_b)

    gather(chunks - 1, rows_b)
    compress(chunks - 2, rows_a)
    for j, part in enumerate(tiles_of(rows_b, tiles, CHUNK - size, size)):
        edge[1, :, j * LANES:(j + 1) * LANES] = part
    compress(chunks - 1, rows_b)

    hs = [pl.ds(h * piece, piece) for h in range(PIECES)]
    for q in range(parts):
        cin[q] = acc[:, q * width:(q + 1) * width].T
    to_core = [[send(cin.at[p ^ (3 - 2 * k), hs[h]], rs1.at[k, hs[h]], core, r_send.at[k, h], r_recv.at[k, h])
                for h in range(PIECES)] for k in range(2)]
    to_far = []
    for h in range(PIECES):
        to_core[0][h].wait_recv()
        stage[hs[h], :] = cin[p ^ 2, hs[h], :] + rs1[0, hs[h], :]
        to_far.append(send(stage.at[hs[h]], rs2.at[hs[h]], far_chip, r_send.at[2, h], r_recv.at[2, h]))
    for copy in to_core[1]:
        copy.wait_recv()
    sent = to_core[0] + to_core[1] + to_far + moved

    in_t.wait()
    in_g.wait()
    for l in range(top):
        wt[l, 0], wt[l, 1] = split(tv[l])
    wf[...] = tv[0]

    def weight(l):
        gh, gl = split(gv[l])
        if l == 0:
            ws[l, 0], ws[l, 1] = gh, gl
            return
        path = stack(wf[...])
        ws[l, 0], ws[l, 1] = split(three(dot, path, gh, gl))
        if l < top:
            wf[...] = three(dot, path, wt[l, 0], wt[l, 1])

    in_k.wait()

    @pl.loop(0, count)
    def _(m):
        pre[m] = jnp.where(tab[1, m] > 0, pre[jnp.maximum(m - 1, 0)], 0.0) + blk[jnp.clip(tab[0, m], 0, count - 1)]

    def near(first, number):
        if not number:
            return

        @pl.loop(first, first + number)
        def _(u):
            none = jnp.zeros((size, size), F32)
            get = lambda r, o: pre[jnp.clip(tab[2, 6 * u + 3 * r + o], 0, count)]
            upper = jnp.concatenate([get(0, 0), get(0, 1), get(0, 2), none], axis=1)
            lower = jnp.concatenate([none, get(1, 0), get(1, 1), get(1, 2)], axis=1)
            band = stack(jnp.concatenate([upper, lower], axis=0))
            at = pl.multiple_of(u * (2 * size), 2 * size)
            span = pl.ds(at, 4 * size)
            nv[pl.ds(at, 2 * size), :] = three(dot, band, ph[span, :], pl_[span, :])

    units = row_blocks // 2
    inner = units - 2
    cuts = [1 + inner * i // (levels + 2) for i in range(levels + 3)]

    def near_step(i):
        near(cuts[i], cuts[i + 1] - cuts[i])

    near_step(0)

    @pl.loop(0, chunks)
    def _(i):
        at = pl.multiple_of(i * CHUNK, CHUNK)
        split_out[pl.ds(2 * at, 2 * CHUNK), :] = stack(bv[pl.ds(at, CHUNK), :])

    for l in range(top):
        moved[l].wait_recv()
        wt[top + l, 0], wt[top + l, 1] = split(tsib[l])

    edges = []
    up = []
    for h in range(PIECES):
        to_far[h].wait_recv()
        cb[0, hs[h], :] = cin[p, hs[h], :] + (rs1[1, hs[h], :] + rs2[hs[h], :])
        up.append(send(cb.at[0, hs[h]], crecv.at[0, hs[h]], siblings[0], c_send.at[0, h], c_recv.at[0, h]))
    for l in range(top):
        if l == 0:
            edges.append(send(edge.at[1], erecv.at[0], following, e_send.at[0], e_recv.at[0]))
            edges.append(send(edge.at[0], erecv.at[1], before, e_send.at[1], e_recv.at[1]))
        own[...] = three(dot, stack(cb[l]), wt[l, 0], wt[l, 1])
        weight(l)
        near_step(1 + l)
        for h in range(PIECES):
            up[l * PIECES + h].wait_recv()
            cb[l + 1, hs[h], :] = own[hs[h], :] + three(dot, stack(crecv[l, hs[h], :]), wt[top + l, 0], wt[top + l, 1])
            up.append(send(cb.at[l + 1, hs[h]], crecv.at[l + 1, hs[h]], siblings[l + 1], c_send.at[l + 1, h], c_recv.at[l + 1, h]))
        part = three(dot_t, stack(crecv[l]), ws[l, 0], ws[l, 1])
        ebuf[...] = part if l == 0 else ebuf[...] + part
    weight(top)
    near_step(levels)
    d0, d1, d2 = [], [], []
    for h in range(PIECES):
        up[top * PIECES + h].wait_recv()
        dbuf[p, hs[h], :] = ebuf[hs[h], :] + three(dot_t, stack(crecv[top, hs[h], :]), ws[top, 0], ws[top, 1])
        mine = dbuf.at[p, hs[h]]
        d0.append(send(mine, mine, far_chip, d_send.at[0, h], d_recv.at[0, h]))
        d1.append(send(mine, mine, core, d_send.at[1, h], d_recv.at[1, h]))

    for copy in edges:
        copy.wait_recv()
    ph[:size, :], pl_[:size, :] = split(jnp.where(p == 0, 0.0, erecv[0]))
    ph[size + rows:, :], pl_[size + rows:, :] = split(jnp.where(p == parts - 1, 0.0, erecv[1]))
    near(0, 1)
    near_step(levels + 1)
    near(units - 1, 1)
    for h in range(PIECES):
        d0[h].wait_recv()
        other = dbuf.at[p ^ 2, hs[h]]
        d2.append(send(other, other, core, d_send.at[2, h], d_recv.at[2, h]))
    for copy in d1 + d2:
        copy.wait_recv()
    for q in range(parts):
        d_out[q * width:(q + 1) * width, :] = dbuf[q]
    for copy in sent + up + edges + d0 + d1 + d2:
        copy.wait_send()


def tree_call(levels, parts, order, pairs, x, basis, blocks, transfer, coupling):
    rows, rank = basis.shape
    tiles = x.shape[0] // rows
    cols = tiles * LANES
    count, size = blocks.shape[0], blocks.shape[1]
    width = cols // parts
    hbm, vmem = (pl.BlockSpec(memory_space=s) for s in (pl.ANY, pltpu.VMEM))
    shape = jax.ShapeDtypeStruct
    dma = pltpu.SemaphoreType.DMA
    part = (width, rank)
    padded = (rows + 2 * size, cols)
    scratch = [
        (x.shape, F32), (basis.shape, F32), ((2 * rank, rows), BF16), ((CHUNK * tiles, LANES), F32), ((CHUNK * tiles, LANES), F32),
        ((rank, cols), F32), ((parts,) + part, F32), ((2, size, cols), F32), (padded, BF16), (padded, BF16),
        (blocks.shape, F32), ((count + 1, size, size), F32),
        (transfer.shape, F32), (coupling.shape, F32), (transfer.shape, F32),
        ((2 * (levels - 1), 2, rank, rank), BF16), ((levels, 2, rank, rank), BF16), ((rank, rank), F32),
        (order.shape, I32), None, ((SUB, LANES), F32), ((SUB, LANES), I32), None,
        ((2,) + part, F32), (part, F32), (part, F32), ((levels,) + part, F32), ((levels,) + part, F32),
        (part, F32), (part, F32), ((parts,) + part, F32), ((2, size, cols), F32),
    ]
    scratch = [pltpu.VMEM(*s) if s else None for s in scratch]
    scratch[19] = pltpu.SMEM(order.shape, I32)
    scratch[22] = pltpu.SMEM((SUB, LANES), I32)
    return pl.pallas_call(
        functools.partial(tree_kernel, levels),
        out_shape=(pltpu.VMEM((cols, rank), F32), pltpu.VMEM((rows, cols), F32), pltpu.VMEM((2 * rows, rank), BF16)),
        in_specs=[vmem, vmem, hbm, hbm, hbm, hbm, hbm],
        out_specs=(vmem, vmem, vmem),
        scratch_shapes=scratch + [
            dma((7,)), dma((levels - 1,)), dma((levels - 1,)), dma((3, PIECES)), dma((3, PIECES)),
            dma((levels, PIECES)), dma((levels, PIECES)), dma((3, PIECES)), dma((3, PIECES)), dma((2,)), dma((2,)),
        ],
        compiler_params=pltpu.CompilerParams(vmem_limit_bytes=48 * MIB, collective_id=0, has_side_effects=True),
        name="tree_near",
    )(order, pairs, x, basis, blocks, transfer, coupling)


def scatter_kernel(order_in, d_in, basis, near, out_hbm, ov, rows_a, rows_b, dh, dl, addr_v, addr, a_sem, out_sem):
    rows, cols = near.shape
    tiles = cols // LANES
    chunks = rows // CHUNK
    addr_v[...] = row_address(order_in[...], tiles)
    in_a = pltpu.make_async_copy(addr_v, addr, a_sem)
    in_a.start()
    for j in range(tiles):
        h, l = split(d_in[j * LANES:(j + 1) * LANES, :].T)
        dh[:, j * LANES:(j + 1) * LANES] = h
        dl[:, j * LANES:(j + 1) * LANES] = l
    in_a.wait()

    def multiply(i, buf):
        at = pl.multiple_of(i * CHUNK, CHUNK)
        total = near[pl.ds(at, CHUNK), :] + three(dot, basis[pl.ds(2 * at, 2 * CHUNK), :], dh[...], dl[...])
        for g in range(CHUNK // SUB):
            for j in range(tiles):
                buf[(g * tiles + j) * SUB:(g * tiles + j + 1) * SUB, :] = total[g * SUB:(g + 1) * SUB, j * LANES:(j + 1) * LANES]

    def scatter(i, buf):
        for k in range(CHUNK):
            to = addr[i * (CHUNK // LANES) + k // LANES, k % LANES]
            ov[pl.ds(to, tiles, stride=SUB), :] = buf[pl.ds((k // SUB) * (SUB * tiles) + k % SUB, tiles, stride=SUB), :]

    multiply(0, rows_a)

    @pl.loop(0, chunks // 2 - 1)
    def _(i):
        multiply(2 * i + 1, rows_b)
        scatter(2 * i, rows_a)
        multiply(2 * i + 2, rows_a)
        scatter(2 * i + 1, rows_b)

    multiply(chunks - 1, rows_b)
    scatter(chunks - 2, rows_a)
    scatter(chunks - 1, rows_b)
    out = pltpu.make_async_copy(ov, out_hbm, out_sem)
    out.start()
    out.wait()


def scatter_call(order, down, basis, near):
    rows, cols = near.shape
    rank = basis.shape[1]
    tiles = cols // LANES
    hbm, vmem = (pl.BlockSpec(memory_space=s) for s in (pl.ANY, pltpu.VMEM))
    return pl.pallas_call(
        scatter_kernel,
        out_shape=jax.ShapeDtypeStruct((rows * tiles, LANES), F32),
        in_specs=[vmem, vmem, vmem, vmem],
        out_specs=hbm,
        scratch_shapes=[
            pltpu.VMEM((rows * tiles, LANES), F32),
            pltpu.VMEM((CHUNK * tiles, LANES), F32), pltpu.VMEM((CHUNK * tiles, LANES), F32),
            pltpu.VMEM((rank, cols), BF16), pltpu.VMEM((rank, cols), BF16),
            pltpu.VMEM(order.shape, I32), pltpu.SMEM(order.shape, I32),
            pltpu.SemaphoreType.DMA, pltpu.SemaphoreType.DMA,
        ],
        compiler_params=pltpu.CompilerParams(vmem_limit_bytes=24 * MIB),
        name="far_scatter",
    )(order, down, basis, near)


def local(points_rhs, order, basis, near_blocks, near_pairs, transfer, coupling):
    rows, cols = points_rhs.shape
    tiles = cols // LANES
    levels = lax.axis_size("leaf").bit_length() - 1
    order = order.reshape(rows // LANES, LANES)
    x = points_rhs.reshape(rows // SUB, SUB, tiles, LANES).transpose(0, 2, 1, 3).reshape(rows * tiles, LANES)
    down, near, halves = tree_call(levels, lax.axis_size("pts"), order, near_pairs.T, x, basis, near_blocks, transfer[0], coupling[0])
    out = scatter_call(order, *(pltpu.with_memory_space_constraint(v, pltpu.VMEM) for v in (down, halves, near)))
    return out.reshape(rows // SUB, tiles, SUB, LANES).transpose(0, 2, 1, 3).reshape(rows, cols)


def solution(mesh):
    return jax.shard_map(
        local,
        mesh=mesh,
        in_specs=(
            P(("leaf", "pts"), None),
            P(("leaf", "pts"), None),
            P(("leaf", "pts"), None),
            P(("leaf", "pts"), None, None),
            P(("leaf", "pts"), None),
            P("leaf", None, None, None),
            P("leaf", None, None, None),
        ),
        out_specs=P(("leaf", "pts"), None),
        check_vma=False,
    )
```

```python
import functools

import jax
import jax.numpy as jnp
from jax import lax
from jax.experimental import pallas as pl
from jax.experimental.pallas import tpu as pltpu
from jax.sharding import PartitionSpec as P

MESH = pl.DeviceIdType.MESH
F32, BF16, I32 = jnp.float32, jnp.bfloat16, jnp.int32
LANES, SUB = 128, 8
MIB = 2**20
CHUNK = 256
PIECES = 4


def split(x):
    hi = x.astype(BF16)
    return hi, (x - hi.astype(F32)).astype(BF16)


def stack(x):
    return jnp.concatenate(split(x), axis=0)


def dot(a, b):
    return jnp.dot(a, b, preferred_element_type=F32)


def dot_t(a, b):
    return lax.dot_general(a, b, (((1,), (1,)), ((), ())), preferred_element_type=F32)


def three(mul, a, bh, bl):
    n = a.shape[0] // 2
    both = mul(a, bh)
    return both[:n] + (both[n:] + mul(a[:n], bl))


def row_address(order, tiles):
    return (order >> 3) * (SUB * tiles) + (order & (SUB - 1))


def tiles_of(ref, tiles, first, count):
    return [
        jnp.concatenate([ref[(g * tiles + j) * SUB:(g * tiles + j + 1) * SUB, :]
                         for g in range(first // SUB, (first + count) // SUB)], axis=0)
        for j in range(tiles)
    ]


def tree_kernel(levels, order_in, pairs_in, x_hbm, basis_hbm, blocks_hbm, t_hbm, g_hbm, d_out, nv, split_out,
                xv, bv, bt, rows_a, rows_b, acc, cin, edge, ph, pl_, blk, pre,
                tv, gv, tsib, wt, ws, wf, addr_v, addr, key_v, tab_v, tab,
                rs1, stage, rs2, cb, crecv, own, eb, cs, prod, erecv,
                in_sem, t_send, t_recv, r_send, r_recv, c_send, c_recv, o_send, o_recv, d_send, d_recv, e_send, e_recv):
    rows, cols = nv.shape
    rank = bv.shape[1]
    tiles = cols // LANES
    count, size = blk.shape[0], blk.shape[1]
    row_blocks = rows // size
    parts, width = cin.shape[:2]
    piece = width // PIECES
    chunks = rows // CHUNK
    leaf, p = lax.axis_index("leaf"), lax.axis_index("pts")
    top = levels - 1
    core, far_chip = (leaf, p ^ 1), (leaf, p ^ 2)
    following, before = (leaf, lax.rem(p + 1, parts)), (leaf, lax.rem(p + parts - 1, parts))
    siblings = [(leaf ^ (1 << l), p) for l in range(levels)]
    across_chip = (leaf ^ (1 << top), p ^ 2)

    def load(src, dst, i):
        copy = pltpu.make_async_copy(src, dst, in_sem.at[i])
        copy.start()
        return copy

    def send(src, dst, to, send_sem, recv_sem):
        copy = pltpu.make_async_remote_copy(
            src_ref=src, dst_ref=dst, send_sem=send_sem, recv_sem=recv_sem, device_id=to, device_id_type=MESH)
        copy.start()
        return copy

    barrier = pltpu.get_barrier_semaphore()
    greeted = [core, far_chip, (leaf, p ^ 3), across_chip] + siblings
    for other in greeted:
        pl.semaphore_signal(barrier, inc=1, device_id=other, device_id_type=MESH)
    addr_v[...] = row_address(order_in[...], tiles)
    in_a = load(addr_v, addr, 5)
    in_b = load(basis_hbm, bv, 2)
    in_x = load(x_hbm, xv, 3)
    in_t = load(t_hbm, tv, 0)
    in_g = load(g_hbm, gv, 1)
    in_k = load(blocks_hbm, blk, 4)

    key_v[...] = jnp.full(key_v.shape, 1e6, F32)
    key_v[0:1, :count] = (2 * pairs_in[0:1, :] + pairs_in[1:2, :]).astype(F32)
    across = jnp.broadcast_to(key_v[0:1, :], (LANES, LANES))
    down_key = across.T
    row_i = lax.broadcasted_iota(I32, (LANES, LANES), 0)
    col_i = lax.broadcasted_iota(I32, (LANES, LANES), 1)
    col_f = col_i.astype(F32)
    one = lambda cond: jnp.where(cond, 1.0, 0.0)
    twin = one((across == down_key) & (col_i < row_i))
    place = jnp.sum(twin + one(across < down_key), axis=1, keepdims=True)
    hit = one(place == col_f)
    again = jnp.where(jnp.sum(twin, axis=1, keepdims=True) > 0, 1.0, 0.0)
    total = lambda x: jnp.sum(x, axis=0, keepdims=True)
    found = total(one(down_key == col_f))
    last = jnp.where(found > 0, total(one(down_key <= col_f)) - 1.0, float(count))
    tab_v[...] = jnp.zeros_like(tab_v)
    tab_v[0:1, :] = total(hit * row_i.astype(F32)).astype(I32)
    tab_v[1:2, :] = total(hit * again).astype(I32)
    tab_v[2:3, :] = last.astype(I32)
    in_tab = load(tab_v, tab, 6)
    pre[0] = jnp.zeros((size, size), F32)
    pre[count] = jnp.zeros((size, size), F32)
    acc[...] = jnp.zeros_like(acc)
    in_b.wait()

    @pl.loop(0, chunks)
    def _(i):
        at = pl.multiple_of(i * CHUNK, CHUNK)
        bt[:, pl.ds(at, CHUNK)] = stack(bv[pl.ds(at, CHUNK), :].T)

    in_a.wait()
    in_tab.wait()
    in_x.wait()

    def gather(i, buf):
        step = 32
        for g in range(CHUNK // step):
            ids = [g * step + u for u in range(step)]
            vals = [xv[pl.ds(addr[i * (CHUNK // LANES) + k // LANES, k % LANES], tiles, stride=SUB), :] for k in ids]
            for k, val in zip(ids, vals):
                buf[pl.ds((k // SUB) * (SUB * tiles) + k % SUB, tiles, stride=SUB), :] = val

    def compress(i, buf):
        at = pl.multiple_of(i * CHUNK, CHUNK)
        hi, lo = zip(*[split(part) for part in tiles_of(buf, tiles, 0, CHUNK)])
        hi, lo = jnp.concatenate(hi, axis=1), jnp.concatenate(lo, axis=1)
        to = pl.ds(pl.multiple_of(size + at, size), CHUNK)
        ph[to, :] = hi
        pl_[to, :] = lo
        acc[...] += three(dot, bt[:, pl.ds(at, CHUNK)], hi, lo)

    gather(0, rows_a)
    pl.semaphore_wait(barrier, len(greeted))
    moved = [send(t_hbm.at[l], tsib.at[l], siblings[l], t_send.at[l], t_recv.at[l]) for l in range(top)]
    for j, part in enumerate(tiles_of(rows_a, tiles, 0, size)):
        edge[0, :, j * LANES:(j + 1) * LANES] = part

    @pl.loop(0, chunks // 2 - 1)
    def _(i):
        gather(2 * i + 1, rows_b)
        compress(2 * i, rows_a)
        gather(2 * i + 2, rows_a)
        compress(2 * i + 1, rows_b)

    gather(chunks - 1, rows_b)
    compress(chunks - 2, rows_a)
    for j, part in enumerate(tiles_of(rows_b, tiles, CHUNK - size, size)):
        edge[1, :, j * LANES:(j + 1) * LANES] = part
    compress(chunks - 1, rows_b)

    hs = [pl.ds(h * piece, piece) for h in range(PIECES)]
    for q in range(parts):
        cin[q] = acc[:, q * width:(q + 1) * width].T
    to_core = [[send(cin.at[p ^ (3 - 2 * k), hs[h]], rs1.at[k, hs[h]], core, r_send.at[k, h], r_recv.at[k, h])
                for h in range(PIECES)] for k in range(2)]
    to_far = []
    for h in range(PIECES):
        to_core[0][h].wait_recv()
        stage[hs[h], :] = cin[p ^ 2, hs[h], :] + rs1[0, hs[h], :]
        to_far.append(send(stage.at[hs[h]], rs2.at[hs[h]], far_chip, r_send.at[2, h], r_recv.at[2, h]))
    for copy in to_core[1]:
        copy.wait_recv()
    sent = to_core[0] + to_core[1] + to_far + moved

    in_t.wait()
    in_g.wait()
    for l in range(top):
        wt[l, 0], wt[l, 1] = split(tv[l])
    wf[...] = tv[0]

    def weight(l):
        gh, gl = split(gv[l])
        if l == 0:
            ws[l, 0], ws[l, 1] = gh, gl
            return
        path = stack(wf[...])
        ws[l, 0], ws[l, 1] = split(three(dot, path, gh, gl))
        if l < top:
            wf[...] = three(dot, path, wt[l, 0], wt[l, 1])

    in_k.wait()

    @pl.loop(0, count)
    def _(m):
        pre[m] = jnp.where(tab[1, m] > 0, pre[jnp.maximum(m - 1, 0)], 0.0) + blk[jnp.clip(tab[0, m], 0, count - 1)]

    def near(first, number):
        if not number:
            return

        @pl.loop(first, first + number)
        def _(u):
            none = jnp.zeros((size, size), F32)
            get = lambda r, o: pre[jnp.clip(tab[2, 6 * u + 3 * r + o], 0, count)]
            upper = jnp.concatenate([get(0, 0), get(0, 1), get(0, 2), none], axis=1)
            lower = jnp.concatenate([none, get(1, 0), get(1, 1), get(1, 2)], axis=1)
            band = stack(jnp.concatenate([upper, lower], axis=0))
            at = pl.multiple_of(u * (2 * size), 2 * size)
            span = pl.ds(at, 4 * size)
            nv[pl.ds(at, 2 * size), :] = three(dot, band, ph[span, :], pl_[span, :])

    units = row_blocks // 2
    inner = units - 2
    cuts = [1 + inner * i // (levels + 2) for i in range(levels + 3)]

    def near_step(i):
        near(cuts[i], cuts[i + 1] - cuts[i])

    near_step(0)

    @pl.loop(0, chunks)
    def _(i):
        at = pl.multiple_of(i * CHUNK, CHUNK)
        split_out[pl.ds(2 * at, 2 * CHUNK), :] = stack(bv[pl.ds(at, CHUNK), :])

    edges = []
    up = []
    over = []
    for h in range(PIECES):
        to_far[h].wait_recv()
        cb[0, hs[h], :] = cin[p, hs[h], :] + (rs1[1, hs[h], :] + rs2[hs[h], :])
        up.append(send(cb.at[0, hs[h]], crecv.at[0, hs[h]], siblings[0], c_send.at[0, h], c_recv.at[0, h]))
    for l in range(top):
        if l == 0:
            edges.append(send(edge.at[1], erecv.at[0], following, e_send.at[0], e_recv.at[0]))
            edges.append(send(edge.at[0], erecv.at[1], before, e_send.at[1], e_recv.at[1]))
        own[...] = three(dot, stack(cb[l]), wt[l, 0], wt[l, 1])
        weight(l)
        near_step(1 + l)
        moved[l].wait_recv()
        wt[top + l, 0], wt[top + l, 1] = split(tsib[l])
        for h in range(PIECES):
            up[l * PIECES + h].wait_recv()
            cb[l + 1, hs[h], :] = own[hs[h], :] + three(dot, stack(crecv[l, hs[h], :]), wt[top + l, 0], wt[top + l, 1])
            mine = cb.at[l + 1, hs[h]]
            to = crecv.at[l + 1, hs[h]] if l + 1 < top else cs.at[p, hs[h]]
            up.append(send(mine, to, siblings[l + 1], c_send.at[l + 1, h], c_recv.at[l + 1, h]))
            if l + 1 == top:
                over.append(send(mine, to, across_chip, o_send.at[h], o_recv.at[h]))
        part = three(dot_t, stack(crecv[l]), ws[l, 0], ws[l, 1])
        eb[p] = part if l == 0 else eb[p] + part

    to_chip = [send(eb.at[p, hs[h]], eb.at[p, hs[h]], far_chip, d_send.at[0, h], d_recv.at[0, h]) for h in range(PIECES)]
    turns = [send(eb.at[p], eb.at[p], core, d_send.at[1, 0], d_recv.at[1, 0])]
    weight(top)
    near_step(levels)
    near_step(levels + 1)

    def lower(q):
        prod[q] = three(dot_t, stack(cs[q]), ws[top, 0], ws[top, 1])

    for k, copies in enumerate((up[top * PIECES:], over)):
        for copy in copies:
            copy.wait_recv()
        turns.append(send(cs.at[p ^ (2 * k)], cs.at[p ^ (2 * k)], core, d_send.at[1, 1 + k], d_recv.at[1, 1 + k]))
        lower(p ^ (2 * k))

    for copy in edges:
        copy.wait_recv()
    ph[:size, :], pl_[:size, :] = split(jnp.where(p == 0, 0.0, erecv[0]))
    ph[size + rows:, :], pl_[size + rows:, :] = split(jnp.where(p == parts - 1, 0.0, erecv[1]))
    near(0, 1)
    near(units - 1, 1)
    for h in range(PIECES):
        to_chip[h].wait_recv()
        other = eb.at[p ^ 2, hs[h]]
        turns.append(send(other, other, core, d_send.at[2, h], d_recv.at[2, h]))
    for k in range(2):
        turns[1 + k].wait_recv()
        lower(p ^ (1 + 2 * k))
    for copy in turns[:1] + turns[3:]:
        copy.wait_recv()
    for q in range(parts):
        d_out[q * width:(q + 1) * width, :] = eb[q] + prod[q]
    for copy in sent + up + over + edges + to_chip + turns:
        copy.wait_send()


def tree_call(levels, parts, order, pairs, x, basis, blocks, transfer, coupling):
    rows, rank = basis.shape
    tiles = x.shape[0] // rows
    cols = tiles * LANES
    count, size = blocks.shape[0], blocks.shape[1]
    width = cols // parts
    hbm, vmem = (pl.BlockSpec(memory_space=s) for s in (pl.ANY, pltpu.VMEM))
    shape = jax.ShapeDtypeStruct
    dma = pltpu.SemaphoreType.DMA
    part = (width, rank)
    padded = (rows + 2 * size, cols)
    scratch = [
        (x.shape, F32), (basis.shape, F32), ((2 * rank, rows), BF16), ((CHUNK * tiles, LANES), F32), ((CHUNK * tiles, LANES), F32),
        ((rank, cols), F32), ((parts,) + part, F32), ((2, size, cols), F32), (padded, BF16), (padded, BF16),
        (blocks.shape, F32), ((count + 1, size, size), F32),
        (transfer.shape, F32), (coupling.shape, F32), (transfer.shape, F32),
        ((2 * (levels - 1), 2, rank, rank), BF16), ((levels, 2, rank, rank), BF16), ((rank, rank), F32),
        (order.shape, I32), None, ((SUB, LANES), F32), ((SUB, LANES), I32), None,
        ((2,) + part, F32), (part, F32), (part, F32), ((levels,) + part, F32), ((levels,) + part, F32),
        (part, F32), ((parts,) + part, F32), ((parts,) + part, F32), ((parts,) + part, F32), ((2, size, cols), F32),
    ]
    scratch = [pltpu.VMEM(*s) if s else None for s in scratch]
    scratch[19] = pltpu.SMEM(order.shape, I32)
    scratch[22] = pltpu.SMEM((SUB, LANES), I32)
    return pl.pallas_call(
        functools.partial(tree_kernel, levels),
        out_shape=(pltpu.VMEM((cols, rank), F32), pltpu.VMEM((rows, cols), F32), pltpu.VMEM((2 * rows, rank), BF16)),
        in_specs=[vmem, vmem, hbm, hbm, hbm, hbm, hbm],
        out_specs=(vmem, vmem, vmem),
        scratch_shapes=scratch + [
            dma((7,)), dma((levels - 1,)), dma((levels - 1,)), dma((3, PIECES)), dma((3, PIECES)),
            dma((levels, PIECES)), dma((levels, PIECES)), dma((PIECES,)), dma((PIECES,)), dma((3, PIECES)), dma((3, PIECES)), dma((2,)), dma((2,)),
        ],
        compiler_params=pltpu.CompilerParams(vmem_limit_bytes=48 * MIB, collective_id=0, has_side_effects=True),
        name="tree_near",
    )(order, pairs, x, basis, blocks, transfer, coupling)


def scatter_kernel(order_in, d_in, basis, near, out_hbm, ov, rows_a, rows_b, dh, dl, addr_v, addr, a_sem, out_sem):
    rows, cols = near.shape
    tiles = cols // LANES
    chunks = rows // CHUNK
    addr_v[...] = row_address(order_in[...], tiles)
    in_a = pltpu.make_async_copy(addr_v, addr, a_sem)
    in_a.start()
    for j in range(tiles):
        h, l = split(d_in[j * LANES:(j + 1) * LANES, :].T)
        dh[:, j * LANES:(j + 1) * LANES] = h
        dl[:, j * LANES:(j + 1) * LANES] = l
    in_a.wait()

    def multiply(i, buf):
        at = pl.multiple_of(i * CHUNK, CHUNK)
        total = near[pl.ds(at, CHUNK), :] + three(dot, basis[pl.ds(2 * at, 2 * CHUNK), :], dh[...], dl[...])
        for g in range(CHUNK // SUB):
            for j in range(tiles):
                buf[(g * tiles + j) * SUB:(g * tiles + j + 1) * SUB, :] = total[g * SUB:(g + 1) * SUB, j * LANES:(j + 1) * LANES]

    def scatter(i, buf):
        for k in range(CHUNK):
            to = addr[i * (CHUNK // LANES) + k // LANES, k % LANES]
            ov[pl.ds(to, tiles, stride=SUB), :] = buf[pl.ds((k // SUB) * (SUB * tiles) + k % SUB, tiles, stride=SUB), :]

    multiply(0, rows_a)

    @pl.loop(0, chunks // 2 - 1)
    def _(i):
        multiply(2 * i + 1, rows_b)
        scatter(2 * i, rows_a)
        multiply(2 * i + 2, rows_a)
        scatter(2 * i + 1, rows_b)

    multiply(chunks - 1, rows_b)
    scatter(chunks - 2, rows_a)
    scatter(chunks - 1, rows_b)
    out = pltpu.make_async_copy(ov, out_hbm, out_sem)
    out.start()
    out.wait()


def scatter_call(order, down, basis, near):
    rows, cols = near.shape
    rank = basis.shape[1]
    tiles = cols // LANES
    hbm, vmem = (pl.BlockSpec(memory_space=s) for s in (pl.ANY, pltpu.VMEM))
    return pl.pallas_call(
        scatter_kernel,
        out_shape=jax.ShapeDtypeStruct((rows * tiles, LANES), F32),
        in_specs=[vmem, vmem, vmem, vmem],
        out_specs=hbm,
        scratch_shapes=[
            pltpu.VMEM((rows * tiles, LANES), F32),
            pltpu.VMEM((CHUNK * tiles, LANES), F32), pltpu.VMEM((CHUNK * tiles, LANES), F32),
            pltpu.VMEM((rank, cols), BF16), pltpu.VMEM((rank, cols), BF16),
            pltpu.VMEM(order.shape, I32), pltpu.SMEM(order.shape, I32),
            pltpu.SemaphoreType.DMA, pltpu.SemaphoreType.DMA,
        ],
        compiler_params=pltpu.CompilerParams(vmem_limit_bytes=24 * MIB),
        name="far_scatter",
    )(order, down, basis, near)


def local(points_rhs, order, basis, near_blocks, near_pairs, transfer, coupling):
    rows, cols = points_rhs.shape
    tiles = cols // LANES
    levels = lax.axis_size("leaf").bit_length() - 1
    order = order.reshape(rows // LANES, LANES)
    x = points_rhs.reshape(rows // SUB, SUB, tiles, LANES).transpose(0, 2, 1, 3).reshape(rows * tiles, LANES)
    down, near, halves = tree_call(levels, lax.axis_size("pts"), order, near_pairs.T, x, basis, near_blocks, transfer[0], coupling[0])
    out = scatter_call(order, *(pltpu.with_memory_space_constraint(v, pltpu.VMEM) for v in (down, halves, near)))
    return out.reshape(rows // SUB, tiles, SUB, LANES).transpose(0, 2, 1, 3).reshape(rows, cols)


def solution(mesh):
    return jax.shard_map(
        local,
        mesh=mesh,
        in_specs=(
            P(("leaf", "pts"), None),
            P(("leaf", "pts"), None),
            P(("leaf", "pts"), None),
            P(("leaf", "pts"), None, None),
            P(("leaf", "pts"), None),
            P("leaf", None, None, None),
            P("leaf", None, None, None),
        ),
        out_specs=P(("leaf", "pts"), None),
        check_vma=False,
    )
```

```python
import functools

import jax
import jax.numpy as jnp
from jax import lax
from jax.experimental import pallas as pl
from jax.experimental.pallas import tpu as pltpu
from jax.sharding import PartitionSpec as P

MESH = pl.DeviceIdType.MESH
F32, BF16, I32 = jnp.float32, jnp.bfloat16, jnp.int32
LANES, SUB = 128, 8
MIB = 2**20
CHUNK = 256
PIECES = 4


def split(x):
    hi = x.astype(BF16)
    return hi, (x - hi.astype(F32)).astype(BF16)


def stack(x):
    return jnp.concatenate(split(x), axis=0)


def dot(a, b):
    return jnp.dot(a, b, preferred_element_type=F32)


def dot_t(a, b):
    return lax.dot_general(a, b, (((1,), (1,)), ((), ())), preferred_element_type=F32)


def three(mul, a, bh, bl):
    n = a.shape[0] // 2
    both = mul(a, bh)
    return both[:n] + (both[n:] + mul(a[:n], bl))


def row_address(order, tiles):
    return (order >> 3) * (SUB * tiles) + (order & (SUB - 1))


def tiles_of(ref, tiles, first, count):
    return [
        jnp.concatenate([ref[(g * tiles + j) * SUB:(g * tiles + j + 1) * SUB, :]
                         for g in range(first // SUB, (first + count) // SUB)], axis=0)
        for j in range(tiles)
    ]


def tree_kernel(levels, order_in, pairs_in, x_hbm, basis_hbm, blocks_hbm, t_hbm, g_hbm, d_out, nv, split_out,
                xv, bv, rows_a, rows_b, acc, cin, edge, ph, pl_, blk, pre,
                tv, gv, tsib, wt, ws, wf, addr_v, addr, key_v, tab_v, tab,
                rs1, stage, rs2, cb, crecv, own, eb, cs, prod, erecv,
                in_sem, t_send, t_recv, r_send, r_recv, c_send, c_recv, o_send, o_recv, d_send, d_recv, e_send, e_recv):
    rows, cols = nv.shape
    rank = bv.shape[1]
    tiles = cols // LANES
    count, size = blk.shape[0], blk.shape[1]
    row_blocks = rows // size
    parts, width = cin.shape[:2]
    piece = width // PIECES
    chunks = rows // CHUNK
    leaf, p = lax.axis_index("leaf"), lax.axis_index("pts")
    top = levels - 1
    core, far_chip = (leaf, p ^ 1), (leaf, p ^ 2)
    following, before = (leaf, lax.rem(p + 1, parts)), (leaf, lax.rem(p + parts - 1, parts))
    siblings = [(leaf ^ (1 << l), p) for l in range(levels)]
    across_chip = (leaf ^ (1 << top), p ^ 2)

    def load(src, dst, i):
        copy = pltpu.make_async_copy(src, dst, in_sem.at[i])
        copy.start()
        return copy

    def send(src, dst, to, send_sem, recv_sem):
        copy = pltpu.make_async_remote_copy(
            src_ref=src, dst_ref=dst, send_sem=send_sem, recv_sem=recv_sem, device_id=to, device_id_type=MESH)
        copy.start()
        return copy

    barrier = pltpu.get_barrier_semaphore()
    greeted = [core, far_chip, (leaf, p ^ 3), across_chip] + siblings
    for other in greeted:
        pl.semaphore_signal(barrier, inc=1, device_id=other, device_id_type=MESH)
    addr_v[...] = row_address(order_in[...], tiles)
    in_a = load(addr_v, addr, 5)
    in_x = load(x_hbm, xv, 3)
    in_b = load(basis_hbm, bv, 2)
    in_t = load(t_hbm, tv, 0)
    in_g = load(g_hbm, gv, 1)
    in_k = load(blocks_hbm, blk, 4)

    key_v[...] = jnp.full(key_v.shape, 1e6, F32)
    key_v[0:1, :count] = (2 * pairs_in[0:1, :] + pairs_in[1:2, :]).astype(F32)
    across = jnp.broadcast_to(key_v[0:1, :], (LANES, LANES))
    down_key = across.T
    row_i = lax.broadcasted_iota(I32, (LANES, LANES), 0)
    col_i = lax.broadcasted_iota(I32, (LANES, LANES), 1)
    col_f = col_i.astype(F32)
    one = lambda cond: jnp.where(cond, 1.0, 0.0)
    twin = one((across == down_key) & (col_i < row_i))
    place = jnp.sum(twin + one(across < down_key), axis=1, keepdims=True)
    hit = one(place == col_f)
    again = jnp.where(jnp.sum(twin, axis=1, keepdims=True) > 0, 1.0, 0.0)
    total = lambda x: jnp.sum(x, axis=0, keepdims=True)
    found = total(one(down_key == col_f))
    last = jnp.where(found > 0, total(one(down_key <= col_f)) - 1.0, float(count))
    tab_v[...] = jnp.zeros_like(tab_v)
    tab_v[0:1, :] = total(hit * row_i.astype(F32)).astype(I32)
    tab_v[1:2, :] = total(hit * again).astype(I32)
    tab_v[2:3, :] = last.astype(I32)
    in_tab = load(tab_v, tab, 6)
    pre[0] = jnp.zeros((size, size), F32)
    pre[count] = jnp.zeros((size, size), F32)
    acc[...] = jnp.zeros_like(acc)
    in_a.wait()
    in_tab.wait()
    in_x.wait()

    def gather(i, buf):
        step = 32
        for g in range(CHUNK // step):
            ids = [g * step + u for u in range(step)]
            vals = [xv[pl.ds(addr[i * (CHUNK // LANES) + k // LANES, k % LANES], tiles, stride=SUB), :] for k in ids]
            for k, val in zip(ids, vals):
                buf[pl.ds((k // SUB) * (SUB * tiles) + k % SUB, tiles, stride=SUB), :] = val

    def compress(i, buf):
        at = pl.multiple_of(i * CHUNK, CHUNK)
        hi, lo = zip(*[split(part) for part in tiles_of(buf, tiles, 0, CHUNK)])
        hi, lo = jnp.concatenate(hi, axis=1), jnp.concatenate(lo, axis=1)
        to = pl.ds(pl.multiple_of(size + at, size), CHUNK)
        ph[to, :] = hi
        pl_[to, :] = lo
        acc[...] += three(dot, stack(bv[pl.ds(at, CHUNK), :].T), hi, lo)

    gather(0, rows_a)
    in_b.wait()
    pl.semaphore_wait(barrier, len(greeted))
    moved = [send(t_hbm.at[l], tsib.at[l], siblings[l], t_send.at[l], t_recv.at[l]) for l in range(top)]
    for j, part in enumerate(tiles_of(rows_a, tiles, 0, size)):
        edge[0, :, j * LANES:(j + 1) * LANES] = part

    @pl.loop(0, chunks // 2 - 1)
    def _(i):
        gather(2 * i + 1, rows_b)
        compress(2 * i, rows_a)
        gather(2 * i + 2, rows_a)
        compress(2 * i + 1, rows_b)

    gather(chunks - 1, rows_b)
    compress(chunks - 2, rows_a)
    for j, part in enumerate(tiles_of(rows_b, tiles, CHUNK - size, size)):
        edge[1, :, j * LANES:(j + 1) * LANES] = part
    compress(chunks - 1, rows_b)

    hs = [pl.ds(h * piece, piece) for h in range(PIECES)]
    to_core = []
    for k, q in enumerate((p ^ 3, p ^ 1, p ^ 2, p)):
        cin[q] = acc[:, pl.ds(pl.multiple_of(q * width, width), width)].T
        if k < 2:
            to_core.append([send(cin.at[q, hs[h]], rs1.at[k, hs[h]], core, r_send.at[k, h], r_recv.at[k, h])
                            for h in range(PIECES)])
    to_far = []
    for h in range(PIECES):
        to_core[0][h].wait_recv()
        stage[hs[h], :] = cin[p ^ 2, hs[h], :] + rs1[0, hs[h], :]
        to_far.append(send(stage.at[hs[h]], rs2.at[hs[h]], far_chip, r_send.at[2, h], r_recv.at[2, h]))
    for copy in to_core[1]:
        copy.wait_recv()
    sent = to_core[0] + to_core[1] + to_far + moved

    in_t.wait()
    in_g.wait()
    for l in range(top):
        wt[l, 0], wt[l, 1] = split(tv[l])
    wf[...] = tv[0]

    def weight(l):
        gh, gl = split(gv[l])
        if l == 0:
            ws[l, 0], ws[l, 1] = gh, gl
            return
        path = stack(wf[...])
        ws[l, 0], ws[l, 1] = split(three(dot, path, gh, gl))
        if l < top:
            wf[...] = three(dot, path, wt[l, 0], wt[l, 1])

    in_k.wait()

    @pl.loop(0, count)
    def _(m):
        pre[m] = jnp.where(tab[1, m] > 0, pre[jnp.maximum(m - 1, 0)], 0.0) + blk[jnp.clip(tab[0, m], 0, count - 1)]

    def near(first, number):
        if not number:
            return

        @pl.loop(first, first + number)
        def _(u):
            none = jnp.zeros((size, size), F32)
            get = lambda r, o: pre[jnp.clip(tab[2, 6 * u + 3 * r + o], 0, count)]
            upper = jnp.concatenate([get(0, 0), get(0, 1), get(0, 2), none], axis=1)
            lower = jnp.concatenate([none, get(1, 0), get(1, 1), get(1, 2)], axis=1)
            band = stack(jnp.concatenate([upper, lower], axis=0))
            at = pl.multiple_of(u * (2 * size), 2 * size)
            span = pl.ds(at, 4 * size)
            nv[pl.ds(at, 2 * size), :] = three(dot, band, ph[span, :], pl_[span, :])

    units = row_blocks // 2
    inner = units - 2
    cuts = [1 + inner * i // (levels + 2) for i in range(levels + 3)]

    def near_step(i):
        near(cuts[i], cuts[i + 1] - cuts[i])

    near_step(0)

    @pl.loop(0, chunks)
    def _(i):
        at = pl.multiple_of(i * CHUNK, CHUNK)
        split_out[pl.ds(2 * at, 2 * CHUNK), :] = stack(bv[pl.ds(at, CHUNK), :])

    edges = []
    up = []
    over = []
    for h in range(PIECES):
        to_far[h].wait_recv()
        cb[0, hs[h], :] = cin[p, hs[h], :] + (rs1[1, hs[h], :] + rs2[hs[h], :])
        up.append(send(cb.at[0, hs[h]], crecv.at[0, hs[h]], siblings[0], c_send.at[0, h], c_recv.at[0, h]))
    for l in range(top):
        if l == 0:
            edges.append(send(edge.at[1], erecv.at[0], following, e_send.at[0], e_recv.at[0]))
            edges.append(send(edge.at[0], erecv.at[1], before, e_send.at[1], e_recv.at[1]))
        own[...] = three(dot, stack(cb[l]), wt[l, 0], wt[l, 1])
        weight(l)
        near_step(1 + l)
        moved[l].wait_recv()
        wt[top + l, 0], wt[top + l, 1] = split(tsib[l])
        for h in range(PIECES):
            up[l * PIECES + h].wait_recv()
            cb[l + 1, hs[h], :] = own[hs[h], :] + three(dot, stack(crecv[l, hs[h], :]), wt[top + l, 0], wt[top + l, 1])
            mine = cb.at[l + 1, hs[h]]
            to = crecv.at[l + 1, hs[h]] if l + 1 < top else cs.at[p, hs[h]]
            up.append(send(mine, to, siblings[l + 1], c_send.at[l + 1, h], c_recv.at[l + 1, h]))
            if l + 1 == top:
                over.append(send(mine, to, across_chip, o_send.at[h], o_recv.at[h]))
        part = three(dot_t, stack(crecv[l]), ws[l, 0], ws[l, 1])
        eb[p] = part if l == 0 else eb[p] + part

    to_chip = [send(eb.at[p, hs[h]], eb.at[p, hs[h]], far_chip, d_send.at[0, h], d_recv.at[0, h]) for h in range(PIECES)]
    turns = [send(eb.at[p], eb.at[p], core, d_send.at[1, 0], d_recv.at[1, 0])]
    weight(top)
    near_step(levels)
    near_step(levels + 1)

    def lower(q):
        prod[q] = three(dot_t, stack(cs[q]), ws[top, 0], ws[top, 1])

    for k, copies in enumerate((up[top * PIECES:], over)):
        for copy in copies:
            copy.wait_recv()
        turns.append(send(cs.at[p ^ (2 * k)], cs.at[p ^ (2 * k)], core, d_send.at[1, 1 + k], d_recv.at[1, 1 + k]))
        lower(p ^ (2 * k))

    for copy in edges:
        copy.wait_recv()
    ph[:size, :], pl_[:size, :] = split(jnp.where(p == 0, 0.0, erecv[0]))
    ph[size + rows:, :], pl_[size + rows:, :] = split(jnp.where(p == parts - 1, 0.0, erecv[1]))
    near(0, 1)
    near(units - 1, 1)
    for h in range(PIECES):
        to_chip[h].wait_recv()
        other = eb.at[p ^ 2, hs[h]]
        turns.append(send(other, other, core, d_send.at[2, h], d_recv.at[2, h]))
    for k in range(2):
        turns[1 + k].wait_recv()
        lower(p ^ (1 + 2 * k))
    for copy in turns[:1] + turns[3:]:
        copy.wait_recv()
    for q in range(parts):
        d_out[q * width:(q + 1) * width, :] = eb[q] + prod[q]
    for copy in sent + up + over + edges + to_chip + turns:
        copy.wait_send()


def tree_call(levels, parts, order, pairs, x, basis, blocks, transfer, coupling):
    rows, rank = basis.shape
    tiles = x.shape[0] // rows
    cols = tiles * LANES
    count, size = blocks.shape[0], blocks.shape[1]
    width = cols // parts
    hbm, vmem = (pl.BlockSpec(memory_space=s) for s in (pl.ANY, pltpu.VMEM))
    shape = jax.ShapeDtypeStruct
    dma = pltpu.SemaphoreType.DMA
    part = (width, rank)
    padded = (rows + 2 * size, cols)
    scratch = [
        (x.shape, F32), (basis.shape, F32), ((CHUNK * tiles, LANES), F32), ((CHUNK * tiles, LANES), F32),
        ((rank, cols), F32), ((parts,) + part, F32), ((2, size, cols), F32), (padded, BF16), (padded, BF16),
        (blocks.shape, F32), ((count + 1, size, size), F32),
        (transfer.shape, F32), (coupling.shape, F32), (transfer.shape, F32),
        ((2 * (levels - 1), 2, rank, rank), BF16), ((levels, 2, rank, rank), BF16), ((rank, rank), F32),
        (order.shape, I32), None, ((SUB, LANES), F32), ((SUB, LANES), I32), None,
        ((2,) + part, F32), (part, F32), (part, F32), ((levels,) + part, F32), ((levels,) + part, F32),
        (part, F32), ((parts,) + part, F32), ((parts,) + part, F32), ((parts,) + part, F32), ((2, size, cols), F32),
    ]
    scratch = [pltpu.VMEM(*s) if s else None for s in scratch]
    scratch[18] = pltpu.SMEM(order.shape, I32)
    scratch[21] = pltpu.SMEM((SUB, LANES), I32)
    return pl.pallas_call(
        functools.partial(tree_kernel, levels),
        out_shape=(pltpu.VMEM((cols, rank), F32), pltpu.VMEM((rows, cols), F32), pltpu.VMEM((2 * rows, rank), BF16)),
        in_specs=[vmem, vmem, hbm, hbm, hbm, hbm, hbm],
        out_specs=(vmem, vmem, vmem),
        scratch_shapes=scratch + [
            dma((7,)), dma((levels - 1,)), dma((levels - 1,)), dma((3, PIECES)), dma((3, PIECES)),
            dma((levels, PIECES)), dma((levels, PIECES)), dma((PIECES,)), dma((PIECES,)), dma((3, PIECES)), dma((3, PIECES)), dma((2,)), dma((2,)),
        ],
        compiler_params=pltpu.CompilerParams(vmem_limit_bytes=48 * MIB, collective_id=0, has_side_effects=True),
        name="tree_near",
    )(order, pairs, x, basis, blocks, transfer, coupling)


def scatter_kernel(order_in, d_in, basis, near, out_hbm, ov, rows_a, rows_b, dh, dl, addr_v, addr, a_sem, out_sem):
    rows, cols = near.shape
    tiles = cols // LANES
    chunks = rows // CHUNK
    addr_v[...] = row_address(order_in[...], tiles)
    in_a = pltpu.make_async_copy(addr_v, addr, a_sem)
    in_a.start()
    for j in range(tiles):
        h, l = split(d_in[j * LANES:(j + 1) * LANES, :].T)
        dh[:, j * LANES:(j + 1) * LANES] = h
        dl[:, j * LANES:(j + 1) * LANES] = l
    in_a.wait()

    def multiply(i, buf):
        at = pl.multiple_of(i * CHUNK, CHUNK)
        total = near[pl.ds(at, CHUNK), :] + three(dot, basis[pl.ds(2 * at, 2 * CHUNK), :], dh[...], dl[...])
        for g in range(CHUNK // SUB):
            for j in range(tiles):
                buf[(g * tiles + j) * SUB:(g * tiles + j + 1) * SUB, :] = total[g * SUB:(g + 1) * SUB, j * LANES:(j + 1) * LANES]

    def scatter(i, buf):
        for k in range(CHUNK):
            to = addr[i * (CHUNK // LANES) + k // LANES, k % LANES]
            ov[pl.ds(to, tiles, stride=SUB), :] = buf[pl.ds((k // SUB) * (SUB * tiles) + k % SUB, tiles, stride=SUB), :]

    multiply(0, rows_a)

    @pl.loop(0, chunks // 2 - 1)
    def _(i):
        multiply(2 * i + 1, rows_b)
        scatter(2 * i, rows_a)
        multiply(2 * i + 2, rows_a)
        scatter(2 * i + 1, rows_b)

    multiply(chunks - 1, rows_b)
    scatter(chunks - 2, rows_a)
    scatter(chunks - 1, rows_b)
    out = pltpu.make_async_copy(ov, out_hbm, out_sem)
    out.start()
    out.wait()


def scatter_call(order, down, basis, near):
    rows, cols = near.shape
    rank = basis.shape[1]
    tiles = cols // LANES
    hbm, vmem = (pl.BlockSpec(memory_space=s) for s in (pl.ANY, pltpu.VMEM))
    return pl.pallas_call(
        scatter_kernel,
        out_shape=jax.ShapeDtypeStruct((rows * tiles, LANES), F32),
        in_specs=[vmem, vmem, vmem, vmem],
        out_specs=hbm,
        scratch_shapes=[
            pltpu.VMEM((rows * tiles, LANES), F32),
            pltpu.VMEM((CHUNK * tiles, LANES), F32), pltpu.VMEM((CHUNK * tiles, LANES), F32),
            pltpu.VMEM((rank, cols), BF16), pltpu.VMEM((rank, cols), BF16),
            pltpu.VMEM(order.shape, I32), pltpu.SMEM(order.shape, I32),
            pltpu.SemaphoreType.DMA, pltpu.SemaphoreType.DMA,
        ],
        compiler_params=pltpu.CompilerParams(vmem_limit_bytes=24 * MIB),
        name="far_scatter",
    )(order, down, basis, near)


def local(points_rhs, order, basis, near_blocks, near_pairs, transfer, coupling):
    rows, cols = points_rhs.shape
    tiles = cols // LANES
    levels = lax.axis_size("leaf").bit_length() - 1
    order = order.reshape(rows // LANES, LANES)
    x = points_rhs.reshape(rows // SUB, SUB, tiles, LANES).transpose(0, 2, 1, 3).reshape(rows * tiles, LANES)
    down, near, halves = tree_call(levels, lax.axis_size("pts"), order, near_pairs.T, x, basis, near_blocks, transfer[0], coupling[0])
    out = scatter_call(order, *(pltpu.with_memory_space_constraint(v, pltpu.VMEM) for v in (down, halves, near)))
    return out.reshape(rows // SUB, tiles, SUB, LANES).transpose(0, 2, 1, 3).reshape(rows, cols)


def solution(mesh):
    return jax.shard_map(
        local,
        mesh=mesh,
        in_specs=(
            P(("leaf", "pts"), None),
            P(("leaf", "pts"), None),
            P(("leaf", "pts"), None),
            P(("leaf", "pts"), None, None),
            P(("leaf", "pts"), None),
            P("leaf", None, None, None),
            P("leaf", None, None, None),
        ),
        out_specs=P(("leaf", "pts"), None),
        check_vma=False,
    )
```

```python
import functools

import jax
import jax.numpy as jnp
from jax import lax
from jax.experimental import pallas as pl
from jax.experimental.pallas import tpu as pltpu
from jax.sharding import PartitionSpec as P

MESH = pl.DeviceIdType.MESH
F32, BF16, I32 = jnp.float32, jnp.bfloat16, jnp.int32
LANES, SUB = 128, 8
MIB = 2**20
CHUNK = 512
PIECES = 4


def split(x):
    hi = x.astype(BF16)
    return hi, (x - hi.astype(F32)).astype(BF16)


def stack(x):
    return jnp.concatenate(split(x), axis=0)


def dot(a, b):
    return jnp.dot(a, b, preferred_element_type=F32)


def dot_t(a, b):
    return lax.dot_general(a, b, (((1,), (1,)), ((), ())), preferred_element_type=F32)


def three(mul, a, bh, bl):
    n = a.shape[0] // 2
    both = mul(a, bh)
    return both[:n] + (both[n:] + mul(a[:n], bl))


def row_address(order, tiles):
    return (order >> 3) * (SUB * tiles) + (order & (SUB - 1))


def tiles_of(ref, tiles, first, count):
    return [
        jnp.concatenate([ref[(g * tiles + j) * SUB:(g * tiles + j + 1) * SUB, :]
                         for g in range(first // SUB, (first + count) // SUB)], axis=0)
        for j in range(tiles)
    ]


def tree_kernel(levels, order_in, pairs_in, x_hbm, basis_hbm, blocks_hbm, t_hbm, g_hbm, d_out, nv, split_out,
                xv, bv, rows_a, rows_b, acc, cin, edge, ph, pl_, blk, pre,
                tv, gv, tsib, wt, ws, wf, addr_v, addr, key_v, tab_v, tab,
                rs1, stage, rs2, cb, crecv, own, eb, cs, prod, erecv,
                in_sem, t_send, t_recv, r_send, r_recv, c_send, c_recv, o_send, o_recv, d_send, d_recv, e_send, e_recv):
    rows, cols = nv.shape
    rank = bv.shape[1]
    tiles = cols // LANES
    count, size = blk.shape[0], blk.shape[1]
    row_blocks = rows // size
    parts, width = cin.shape[:2]
    piece = width // PIECES
    chunks = rows // CHUNK
    leaf, p = lax.axis_index("leaf"), lax.axis_index("pts")
    top = levels - 1
    core, far_chip = (leaf, p ^ 1), (leaf, p ^ 2)
    following, before = (leaf, lax.rem(p + 1, parts)), (leaf, lax.rem(p + parts - 1, parts))
    siblings = [(leaf ^ (1 << l), p) for l in range(levels)]
    across_chip = (leaf ^ (1 << top), p ^ 2)

    def load(src, dst, i):
        copy = pltpu.make_async_copy(src, dst, in_sem.at[i])
        copy.start()
        return copy

    def send(src, dst, to, send_sem, recv_sem):
        copy = pltpu.make_async_remote_copy(
            src_ref=src, dst_ref=dst, send_sem=send_sem, recv_sem=recv_sem, device_id=to, device_id_type=MESH)
        copy.start()
        return copy

    barrier = pltpu.get_barrier_semaphore()
    greeted = [core, far_chip, (leaf, p ^ 3), across_chip] + siblings
    for other in greeted:
        pl.semaphore_signal(barrier, inc=1, device_id=other, device_id_type=MESH)
    addr_v[...] = row_address(order_in[...], tiles)
    in_a = load(addr_v, addr, 5)
    in_x = load(x_hbm, xv, 3)
    in_b = load(basis_hbm, bv, 2)
    in_t = load(t_hbm, tv, 0)
    in_g = load(g_hbm, gv, 1)
    in_k = load(blocks_hbm, blk, 4)

    key_v[...] = jnp.full(key_v.shape, 1e6, F32)
    key_v[0:1, :count] = (2 * pairs_in[0:1, :] + pairs_in[1:2, :]).astype(F32)
    across = jnp.broadcast_to(key_v[0:1, :], (LANES, LANES))
    down_key = across.T
    row_i = lax.broadcasted_iota(I32, (LANES, LANES), 0)
    col_i = lax.broadcasted_iota(I32, (LANES, LANES), 1)
    col_f = col_i.astype(F32)
    one = lambda cond: jnp.where(cond, 1.0, 0.0)
    twin = one((across == down_key) & (col_i < row_i))
    place = jnp.sum(twin + one(across < down_key), axis=1, keepdims=True)
    hit = one(place == col_f)
    again = jnp.where(jnp.sum(twin, axis=1, keepdims=True) > 0, 1.0, 0.0)
    total = lambda x: jnp.sum(x, axis=0, keepdims=True)
    found = total(one(down_key == col_f))
    last = jnp.where(found > 0, total(one(down_key <= col_f)) - 1.0, float(count))
    tab_v[...] = jnp.zeros_like(tab_v)
    tab_v[0:1, :] = total(hit * row_i.astype(F32)).astype(I32)
    tab_v[1:2, :] = total(hit * again).astype(I32)
    tab_v[2:3, :] = last.astype(I32)
    in_tab = load(tab_v, tab, 6)
    pre[0] = jnp.zeros((size, size), F32)
    pre[count] = jnp.zeros((size, size), F32)
    acc[...] = jnp.zeros_like(acc)
    in_a.wait()
    in_tab.wait()
    in_x.wait()

    def gather(i, buf):
        step = 32
        for g in range(CHUNK // step):
            ids = [g * step + u for u in range(step)]
            vals = [xv[pl.ds(addr[i * (CHUNK // LANES) + k // LANES, k % LANES], tiles, stride=SUB), :] for k in ids]
            for k, val in zip(ids, vals):
                buf[pl.ds((k // SUB) * (SUB * tiles) + k % SUB, tiles, stride=SUB), :] = val

    def compress(i, buf):
        at = pl.multiple_of(i * CHUNK, CHUNK)
        hi, lo = zip(*[split(part) for part in tiles_of(buf, tiles, 0, CHUNK)])
        hi, lo = jnp.concatenate(hi, axis=1), jnp.concatenate(lo, axis=1)
        to = pl.ds(pl.multiple_of(size + at, size), CHUNK)
        ph[to, :] = hi
        pl_[to, :] = lo
        acc[...] += three(dot, stack(bv[pl.ds(at, CHUNK), :].T), hi, lo)

    gather(0, rows_a)
    pl.semaphore_wait(barrier, len(greeted))
    moved = [send(t_hbm.at[l], tsib.at[l], siblings[l], t_send.at[l], t_recv.at[l]) for l in range(top)]
    for j, part in enumerate(tiles_of(rows_a, tiles, 0, size)):
        edge[0, :, j * LANES:(j + 1) * LANES] = part

    in_b.wait()

    @pl.loop(0, chunks // 2 - 1)
    def _(i):
        gather(2 * i + 1, rows_b)
        compress(2 * i, rows_a)
        gather(2 * i + 2, rows_a)
        compress(2 * i + 1, rows_b)

    gather(chunks - 1, rows_b)
    compress(chunks - 2, rows_a)
    for j, part in enumerate(tiles_of(rows_b, tiles, CHUNK - size, size)):
        edge[1, :, j * LANES:(j + 1) * LANES] = part
    compress(chunks - 1, rows_b)

    hs = [pl.ds(h * piece, piece) for h in range(PIECES)]
    to_core = []
    for k, q in enumerate((p ^ 3, p ^ 1, p ^ 2, p)):
        cin[q] = acc[:, pl.ds(pl.multiple_of(q * width, width), width)].T
        if k < 2:
            to_core.append([send(cin.at[q, hs[h]], rs1.at[k, hs[h]], core, r_send.at[k, h], r_recv.at[k, h])
                            for h in range(PIECES)])
    to_far = []
    for h in range(PIECES):
        to_core[0][h].wait_recv()
        stage[hs[h], :] = cin[p ^ 2, hs[h], :] + rs1[0, hs[h], :]
        to_far.append(send(stage.at[hs[h]], rs2.at[hs[h]], far_chip, r_send.at[2, h], r_recv.at[2, h]))
    for copy in to_core[1]:
        copy.wait_recv()
    sent = to_core[0] + to_core[1] + to_far + moved

    in_t.wait()
    in_g.wait()
    for l in range(top):
        wt[l, 0], wt[l, 1] = split(tv[l])
    wf[...] = tv[0]

    def weight(l):
        gh, gl = split(gv[l])
        if l == 0:
            ws[l, 0], ws[l, 1] = gh, gl
            return
        path = stack(wf[...])
        ws[l, 0], ws[l, 1] = split(three(dot, path, gh, gl))
        if l < top:
            wf[...] = three(dot, path, wt[l, 0], wt[l, 1])

    in_k.wait()

    @pl.loop(0, count)
    def _(m):
        pre[m] = jnp.where(tab[1, m] > 0, pre[jnp.maximum(m - 1, 0)], 0.0) + blk[jnp.clip(tab[0, m], 0, count - 1)]

    def near(first, number):
        if not number:
            return

        @pl.loop(first, first + number)
        def _(u):
            none = jnp.zeros((size, size), F32)
            get = lambda r, o: pre[jnp.clip(tab[2, 6 * u + 3 * r + o], 0, count)]
            upper = jnp.concatenate([get(0, 0), get(0, 1), get(0, 2), none], axis=1)
            lower = jnp.concatenate([none, get(1, 0), get(1, 1), get(1, 2)], axis=1)
            band = stack(jnp.concatenate([upper, lower], axis=0))
            at = pl.multiple_of(u * (2 * size), 2 * size)
            span = pl.ds(at, 4 * size)
            nv[pl.ds(at, 2 * size), :] = three(dot, band, ph[span, :], pl_[span, :])

    units = row_blocks // 2
    inner = units - 2
    cuts = [1 + inner * i // (levels + 2) for i in range(levels + 3)]

    def near_step(i):
        near(cuts[i], cuts[i + 1] - cuts[i])

    near_step(0)

    @pl.loop(0, chunks)
    def _(i):
        at = pl.multiple_of(i * CHUNK, CHUNK)
        split_out[pl.ds(2 * at, 2 * CHUNK), :] = stack(bv[pl.ds(at, CHUNK), :])

    edges = []
    up = []
    over = []
    for h in range(PIECES):
        to_far[h].wait_recv()
        cb[0, hs[h], :] = cin[p, hs[h], :] + (rs1[1, hs[h], :] + rs2[hs[h], :])
        up.append(send(cb.at[0, hs[h]], crecv.at[0, hs[h]], siblings[0], c_send.at[0, h], c_recv.at[0, h]))
    for l in range(top):
        if l == 0:
            edges.append(send(edge.at[1], erecv.at[0], following, e_send.at[0], e_recv.at[0]))
            edges.append(send(edge.at[0], erecv.at[1], before, e_send.at[1], e_recv.at[1]))
        own[...] = three(dot, stack(cb[l]), wt[l, 0], wt[l, 1])
        weight(l)
        near_step(1 + l)
        moved[l].wait_recv()
        wt[top + l, 0], wt[top + l, 1] = split(tsib[l])
        for h in range(PIECES):
            up[l * PIECES + h].wait_recv()
            cb[l + 1, hs[h], :] = own[hs[h], :] + three(dot, stack(crecv[l, hs[h], :]), wt[top + l, 0], wt[top + l, 1])
            mine = cb.at[l + 1, hs[h]]
            to = crecv.at[l + 1, hs[h]] if l + 1 < top else cs.at[p, hs[h]]
            up.append(send(mine, to, siblings[l + 1], c_send.at[l + 1, h], c_recv.at[l + 1, h]))
            if l + 1 == top:
                over.append(send(mine, to, across_chip, o_send.at[h], o_recv.at[h]))
        part = three(dot_t, stack(crecv[l]), ws[l, 0], ws[l, 1])
        eb[p] = part if l == 0 else eb[p] + part

    to_chip = [send(eb.at[p, hs[h]], eb.at[p, hs[h]], far_chip, d_send.at[0, h], d_recv.at[0, h]) for h in range(PIECES)]
    turns = [send(eb.at[p], eb.at[p], core, d_send.at[1, 0], d_recv.at[1, 0])]
    weight(top)
    near_step(levels)
    near_step(levels + 1)

    def lower(q):
        prod[q] = three(dot_t, stack(cs[q]), ws[top, 0], ws[top, 1])

    for k, copies in enumerate((up[top * PIECES:], over)):
        for copy in copies:
            copy.wait_recv()
        turns.append(send(cs.at[p ^ (2 * k)], cs.at[p ^ (2 * k)], core, d_send.at[1, 1 + k], d_recv.at[1, 1 + k]))
        lower(p ^ (2 * k))

    for copy in edges:
        copy.wait_recv()
    ph[:size, :], pl_[:size, :] = split(jnp.where(p == 0, 0.0, erecv[0]))
    ph[size + rows:, :], pl_[size + rows:, :] = split(jnp.where(p == parts - 1, 0.0, erecv[1]))
    near(0, 1)
    near(units - 1, 1)
    for h in range(PIECES):
        to_chip[h].wait_recv()
        other = eb.at[p ^ 2, hs[h]]
        turns.append(send(other, other, core, d_send.at[2, h], d_recv.at[2, h]))
    for k in range(2):
        turns[1 + k].wait_recv()
        lower(p ^ (1 + 2 * k))
    for copy in turns[:1] + turns[3:]:
        copy.wait_recv()
    for q in range(parts):
        d_out[q * width:(q + 1) * width, :] = eb[q] + prod[q]
    for copy in sent + up + over + edges + to_chip + turns:
        copy.wait_send()


def tree_call(levels, parts, order, pairs, x, basis, blocks, transfer, coupling):
    rows, rank = basis.shape
    tiles = x.shape[0] // rows
    cols = tiles * LANES
    count, size = blocks.shape[0], blocks.shape[1]
    width = cols // parts
    hbm, vmem = (pl.BlockSpec(memory_space=s) for s in (pl.ANY, pltpu.VMEM))
    shape = jax.ShapeDtypeStruct
    dma = pltpu.SemaphoreType.DMA
    part = (width, rank)
    padded = (rows + 2 * size, cols)
    scratch = [
        (x.shape, F32), (basis.shape, F32), ((CHUNK * tiles, LANES), F32), ((CHUNK * tiles, LANES), F32),
        ((rank, cols), F32), ((parts,) + part, F32), ((2, size, cols), F32), (padded, BF16), (padded, BF16),
        (blocks.shape, F32), ((count + 1, size, size), F32),
        (transfer.shape, F32), (coupling.shape, F32), (transfer.shape, F32),
        ((2 * (levels - 1), 2, rank, rank), BF16), ((levels, 2, rank, rank), BF16), ((rank, rank), F32),
        (order.shape, I32), None, ((SUB, LANES), F32), ((SUB, LANES), I32), None,
        ((2,) + part, F32), (part, F32), (part, F32), ((levels,) + part, F32), ((levels,) + part, F32),
        (part, F32), ((parts,) + part, F32), ((parts,) + part, F32), ((parts,) + part, F32), ((2, size, cols), F32),
    ]
    scratch = [pltpu.VMEM(*s) if s else None for s in scratch]
    scratch[18] = pltpu.SMEM(order.shape, I32)
    scratch[21] = pltpu.SMEM((SUB, LANES), I32)
    return pl.pallas_call(
        functools.partial(tree_kernel, levels),
        out_shape=(pltpu.VMEM((cols, rank), F32), pltpu.VMEM((rows, cols), F32), pltpu.VMEM((2 * rows, rank), BF16)),
        in_specs=[vmem, vmem, hbm, hbm, hbm, hbm, hbm],
        out_specs=(vmem, vmem, vmem),
        scratch_shapes=scratch + [
            dma((7,)), dma((levels - 1,)), dma((levels - 1,)), dma((3, PIECES)), dma((3, PIECES)),
            dma((levels, PIECES)), dma((levels, PIECES)), dma((PIECES,)), dma((PIECES,)), dma((3, PIECES)), dma((3, PIECES)), dma((2,)), dma((2,)),
        ],
        compiler_params=pltpu.CompilerParams(vmem_limit_bytes=48 * MIB, collective_id=0, has_side_effects=True),
        name="tree_near",
    )(order, pairs, x, basis, blocks, transfer, coupling)


def scatter_kernel(order_in, d_in, basis, near, out_hbm, ov, rows_a, rows_b, dh, dl, addr_v, addr, a_sem, out_sem):
    rows, cols = near.shape
    tiles = cols // LANES
    chunks = rows // CHUNK
    addr_v[...] = row_address(order_in[...], tiles)
    in_a = pltpu.make_async_copy(addr_v, addr, a_sem)
    in_a.start()
    for j in range(tiles):
        h, l = split(d_in[j * LANES:(j + 1) * LANES, :].T)
        dh[:, j * LANES:(j + 1) * LANES] = h
        dl[:, j * LANES:(j + 1) * LANES] = l
    in_a.wait()

    def multiply(i, buf):
        at = pl.multiple_of(i * CHUNK, CHUNK)
        total = near[pl.ds(at, CHUNK), :] + three(dot, basis[pl.ds(2 * at, 2 * CHUNK), :], dh[...], dl[...])
        for g in range(CHUNK // SUB):
            for j in range(tiles):
                buf[(g * tiles + j) * SUB:(g * tiles + j + 1) * SUB, :] = total[g * SUB:(g + 1) * SUB, j * LANES:(j + 1) * LANES]

    def scatter(i, buf):
        for k in range(CHUNK):
            to = addr[i * (CHUNK // LANES) + k // LANES, k % LANES]
            ov[pl.ds(to, tiles, stride=SUB), :] = buf[pl.ds((k // SUB) * (SUB * tiles) + k % SUB, tiles, stride=SUB), :]

    multiply(0, rows_a)

    @pl.loop(0, chunks // 2 - 1)
    def _(i):
        multiply(2 * i + 1, rows_b)
        scatter(2 * i, rows_a)
        multiply(2 * i + 2, rows_a)
        scatter(2 * i + 1, rows_b)

    multiply(chunks - 1, rows_b)
    scatter(chunks - 2, rows_a)
    scatter(chunks - 1, rows_b)
    out = pltpu.make_async_copy(ov, out_hbm, out_sem)
    out.start()
    out.wait()


def scatter_call(order, down, basis, near):
    rows, cols = near.shape
    rank = basis.shape[1]
    tiles = cols // LANES
    hbm, vmem = (pl.BlockSpec(memory_space=s) for s in (pl.ANY, pltpu.VMEM))
    return pl.pallas_call(
        scatter_kernel,
        out_shape=jax.ShapeDtypeStruct((rows * tiles, LANES), F32),
        in_specs=[vmem, vmem, vmem, vmem],
        out_specs=hbm,
        scratch_shapes=[
            pltpu.VMEM((rows * tiles, LANES), F32),
            pltpu.VMEM((CHUNK * tiles, LANES), F32), pltpu.VMEM((CHUNK * tiles, LANES), F32),
            pltpu.VMEM((rank, cols), BF16), pltpu.VMEM((rank, cols), BF16),
            pltpu.VMEM(order.shape, I32), pltpu.SMEM(order.shape, I32),
            pltpu.SemaphoreType.DMA, pltpu.SemaphoreType.DMA,
        ],
        compiler_params=pltpu.CompilerParams(vmem_limit_bytes=24 * MIB),
        name="far_scatter",
    )(order, down, basis, near)


def local(points_rhs, order, basis, near_blocks, near_pairs, transfer, coupling):
    rows, cols = points_rhs.shape
    tiles = cols // LANES
    levels = lax.axis_size("leaf").bit_length() - 1
    order = order.reshape(rows // LANES, LANES)
    x = points_rhs.reshape(rows // SUB, SUB, tiles, LANES).transpose(0, 2, 1, 3).reshape(rows * tiles, LANES)
    down, near, halves = tree_call(levels, lax.axis_size("pts"), order, near_pairs.T, x, basis, near_blocks, transfer[0], coupling[0])
    out = scatter_call(order, *(pltpu.with_memory_space_constraint(v, pltpu.VMEM) for v in (down, halves, near)))
    return out.reshape(rows // SUB, tiles, SUB, LANES).transpose(0, 2, 1, 3).reshape(rows, cols)


def solution(mesh):
    return jax.shard_map(
        local,
        mesh=mesh,
        in_specs=(
            P(("leaf", "pts"), None),
            P(("leaf", "pts"), None),
            P(("leaf", "pts"), None),
            P(("leaf", "pts"), None, None),
            P(("leaf", "pts"), None),
            P("leaf", None, None, None),
            P("leaf", None, None, None),
        ),
        out_specs=P(("leaf", "pts"), None),
        check_vma=False,
    )
```
